128 devices in a mesh: lat: 16 (over z, x), lon: 8 (over y, core).
Axes of the slice: x: 4, y: 4, z: 4, core: 2. Of those that a mesh axis runs over, the one named last changes fastest.
Arguments:
- adjoint_grid: float32 [1280, 8, 3072], P('lat', None, 'lon'), may hold values from -6 to 6
- tile_owner: int32 [16, 8, 240, 1], P('lat', 'lon'), may hold values from 0 to 127, as said below
- tile_slot: int32 [16, 8, 240, 1], P('lat', 'lon'), may hold values from 0 to 239
- stencil: int32 [1280, 24, 4, 128], P('lat', 'lon'), may hold values from 0 to 127
- interp_weight: float32 [1280, 24, 4, 128], P('lat', 'lon'), may hold values from 0 to 0.5
- vertical_offset: float32 [1280, 4, 2, 2], P('lat'), may hold values from -0.6 to 0.6
- diffusion_rate: float32 [8], replicated, may hold values from 1 to 1000
Outputs:
- adjoint_out: float32 [1280, 8, 3072], P('lat', None, 'lon')
The draws below stay inside these ranges and needn't reach their ends.
Inputs may be any that keep to these rules, and one draw needn't show every extreme that they name: `tile_owner`: A device is named as its latitude band times the number of longitude bands plus its longitude band. A tile of band pair (a, b) names a band pair (a + da, (b + db) mod the number of longitude bands) with da and db in -1, 0, 1 and a + da a valid latitude band: its own pair or one of its neighbours, longitude wrapping around. Among the 240 tiles of one band pair, no band pair is named more than 80 times, and every band pair names some band pair exactly 80 times.
All inputs are finite; a program needn't handle non-finite values.
Results may differ from the reference program's by a relative error of at most 0.00055.
Values sent between devices are 32-bit elements; how exact they have to be, the bound alone decides.
No kernel may reach another device: no remote copies, remote signals or barrier semaphores. Data moves between devices by JAX's collectives and lax.ppermute only.
A program may use at most 256 MiB of HBM per device.

```python
import math
import jax
import jax.numpy as jnp
from jax import lax

NLAT = 1280
NLON = 3072
NM = 640
FIELDS = 4
LEV = 2
TILE = 128
STEN = 4
FL = 8
LAT_DEV = 80
TPR = 3
TILES = 240
CAP = 80
M_DEV = 40
N_LAT = 16
N_LON = 8


def owner_of_pair(pair_key, lat_band, lon_band):
    key_order, key_share, key_shuffle = jax.random.split(pair_key, 3)
    order = jax.random.permutation(key_order, jnp.arange(9, dtype=jnp.int32))
    lat_step = order // 3 - 1
    lon_step = order % 3 - 1
    target_lat = lat_band + lat_step
    valid = (target_lat >= 0) & (target_lat < N_LAT)
    shares = jax.random.randint(key_share, (9,), CAP // 2, CAP + 1, dtype=jnp.int32)
    leading = valid & (jnp.cumsum(valid.astype(jnp.int32)) == 1)
    shares = jnp.where(leading, CAP, jnp.where(valid, shares, 0)).astype(jnp.int32)
    ends = jnp.cumsum(shares)
    tile_ids = jax.random.permutation(key_shuffle, jnp.arange(TILES, dtype=jnp.int32))
    which = jnp.sum((tile_ids[:, None] >= ends[None, :]).astype(jnp.int32), axis=1)
    chosen_lat = target_lat[which]
    chosen_lon = (lon_band + lon_step[which] + N_LON) % N_LON
    return (chosen_lat * N_LON + chosen_lon).astype(jnp.int32)


def draw_tile_owner(key, part):
    pair_keys = jax.random.split(key, N_LAT * N_LON)
    pair_ids = jnp.arange(N_LAT * N_LON, dtype=jnp.int32)
    owners = jax.vmap(owner_of_pair)(pair_keys, pair_ids // N_LON, pair_ids % N_LON)
    return owners.reshape(N_LAT, N_LON, TILES, 1)


def touch_ends(values, own_key, least, largest):
    dims = values.shape
    place = [jax.random.randint(jax.random.fold_in(own_key, axis), (), 0, dims[axis]) for axis in range(len(dims))]
    values = values.at[tuple(place)].set(least)
    longest = dims.index(max(dims))
    place[longest] = (place[longest] + 1) % dims[longest]
    return values.at[tuple(place)].set(largest)


def shard_levels(stream_key, shape, pieces, low, high):
    def one(position, blocks):
        heights = jax.random.uniform(jax.random.fold_in(jax.random.fold_in(stream_key, 6), position), (blocks,), jnp.float32, low / len(pieces), high / len(pieces))
        return jnp.repeat(jnp.exp(heights), shape[position] // blocks).reshape((-1,) + (1,) * (len(shape) - position - 1))

    loudness = one(*pieces[0])
    for cut in pieces[1:]:
        loudness = loudness * one(*cut)
    return loudness


def centred(stream_key, shape, scale, reach, cuts=(), held_as=jnp.bfloat16):
    drawn = scale * jax.random.normal(stream_key, shape, jnp.float32)
    if cuts:
        drawn = drawn * shard_levels(stream_key, shape, cuts, -0.22, 0.18)
    return jnp.clip(drawn, -reach, reach).astype(held_as)


def setup_inputs(seed: int = 0) -> dict:
    seeds = jax.random.split(jax.random.key(seed), 8)
    adjoint_grid = centred(seeds[0], (NLAT, FL, NLON), 1.0, 6.0, ((0, 16), (2, 8)), jnp.float32)
    tile_owner = draw_tile_owner(jax.random.fold_in(seeds[7], 71), 0)
    tile_slot = touch_ends(jax.random.randint(seeds[2], (N_LAT, N_LON, TILES, 1), 0, TILES), jax.random.fold_in(seeds[2], 1), 0, TILES - 1).astype(jnp.int32)
    stencil = touch_ends(jax.random.randint(seeds[3], (NLAT, NLON // TILE, STEN, TILE), 0, TILE), jax.random.fold_in(seeds[3], 1), 0, TILE - 1).astype(jnp.int32)
    interp_weight = jnp.clip(0.5 * jax.random.uniform(seeds[4], (NLAT, NLON // TILE, STEN, TILE), jnp.float32) ** shard_levels(seeds[4], (NLAT, NLON // TILE, STEN, TILE), ((0, 16), (1, 8)), -0.2, 0.2), 0.0, 0.5)
    vertical_offset = centred(seeds[5], (NLAT, FIELDS, LEV, LEV), 0.1, 0.6, ((0, 16),), jnp.float32)
    diffusion_rate = jnp.clip(jnp.exp(jax.random.uniform(seeds[6], (FL,), jnp.float32, math.log(1.0), math.log(1000.0))), 1.0, 1000.0)
    return {"adjoint_grid": adjoint_grid, "tile_owner": tile_owner, "tile_slot": tile_slot, "stencil": stencil, "interp_weight": interp_weight, "vertical_offset": vertical_offset, "diffusion_rate": diffusion_rate}


highest = lax.Precision.HIGHEST
gamma_shift = 0.5 * math.log(math.pi)
log_floor = -60.0

def fourier_table(point_count, wave_total, block_count):
    per_block = wave_total // block_count
    column = jnp.arange(2 * wave_total, dtype=jnp.int32)
    wave_ids = column // (2 * per_block) * per_block + column % per_block
    part_ids = column // per_block % 2
    points = jnp.arange(point_count, dtype=jnp.int32)
    phase_ids = points[:, None] * wave_ids[None, :] % point_count
    angles = phase_ids.astype(jnp.float32) * (2.0 * math.pi / point_count)
    return (jnp.where(part_ids[None, :] == 0, jnp.cos(angles), -jnp.sin(angles)), wave_ids)

def latitude_rows(lat_total, row_count):
    rows_f = jnp.arange(row_count, dtype=jnp.int32).astype(jnp.float32)
    latitude = 0.5 * math.pi - math.pi * (rows_f + 0.5) / lat_total
    return (jnp.sin(latitude), jnp.cos(latitude))

def legendre_diagonal(order_f, cos_lat):
    log_norm = 0.5 * (lax.lgamma(order_f + 1.5) - lax.lgamma(order_f + 1.0) - gamma_shift)
    exponent = log_norm + order_f * jnp.log(cos_lat)[None, :]
    kept = exponent >= log_floor
    return jnp.where(kept, jnp.exp(jnp.where(kept, exponent, 0.0)), 0.0)

def legendre_scan(recurrence, first_degree, degree_count, wave_ids, order_f, sine_lat, diagonal):

    def advance(carried, degree):
        previous, earlier, scale_prev = carried
        degree_f = degree.astype(jnp.float32)
        scale_now = jnp.sqrt(jnp.maximum(4.0 * degree_f * degree_f - 1.0, 1.0) / jnp.maximum(degree_f * degree_f - order_f * order_f, 1.0))
        stepped = scale_now * (sine_lat[None, :] * previous - earlier / scale_prev)
        current = jnp.where(degree < wave_ids[:, None], 0.0, jnp.where(degree == wave_ids[:, None], diagonal, stepped))
        return ((current, previous, scale_now), current)
    degrees = first_degree + jnp.arange(degree_count, dtype=jnp.int32)
    return lax.scan(advance, recurrence, degrees, unroll=8)

def damping(local_rates, degrees):
    degree_f = degrees.astype(jnp.float32)
    ratio = local_rates[:, None] * (degree_f * (degree_f + 1.0) / float(NM * (NM + 1)))[None, :]
    return -ratio / (1.0 + ratio)

def spread_tiles(field, stencil, interp_weight):
    row_count, fields_levels, lon_width = field.shape
    tiles_row, stencil_count, tile_width = (stencil.shape[1], stencil.shape[2], stencil.shape[3])
    tiled = field.reshape(row_count, fields_levels, tiles_row, tile_width)
    targets = jnp.arange(tile_width, dtype=jnp.int32)
    spread_map = jnp.zeros((row_count, tiles_row, tile_width, tile_width), jnp.float32)
    for stencil_id in range(stencil_count):
        spread_map = spread_map + jnp.where(stencil[:, :, stencil_id, :, None] == targets, interp_weight[:, :, stencil_id, :, None], 0.0)
    return jnp.einsum('rfkp,rkpq->rkfq', tiled, spread_map, precision=highest)

def vertical_mix(field, offset):
    row_count, fields_levels, lon_width = field.shape
    layered = field.reshape(row_count, offset.shape[1], offset.shape[2], lon_width)
    mixed = layered + jnp.einsum('rilk,rilx->rikx', offset, layered, precision=highest)
    return mixed.reshape(row_count, fields_levels, lon_width)

def lagrangian_adjoint(field, tile_owner, tile_slot, stencil, interp_weight):
    tile_cols = NLON // TILE
    band_field = field.reshape(N_LAT, LAT_DEV, FL, NLON)
    band_stencil = stencil.reshape(N_LAT, LAT_DEV, tile_cols, STEN, TILE)
    band_weight = interp_weight.reshape(N_LAT, LAT_DEV, tile_cols, STEN, TILE)

    def one_band(packed):
        return spread_tiles(packed[0], packed[1], packed[2])
    spread = lax.map(one_band, (band_field, band_stencil, band_weight))
    row_ids = jnp.arange(NLAT, dtype=jnp.int32)[:, None]
    col_ids = jnp.arange(tile_cols, dtype=jnp.int32)[None, :]
    lat_band = row_ids // LAT_DEV
    lon_band = col_ids // TPR
    local_ids = row_ids % LAT_DEV * TPR + col_ids % TPR
    owners = tile_owner[lat_band, lon_band, local_ids, 0]
    slot_ids = tile_slot[lat_band, lon_band, local_ids, 0]
    dest_row = owners // N_LON * LAT_DEV + slot_ids // TPR
    dest_col = owners % N_LON * TPR + slot_ids % TPR
    dest_ids = (dest_row * tile_cols + dest_col).reshape(NLAT * tile_cols).astype(jnp.int32)
    summed = jax.ops.segment_sum(spread.reshape(NLAT * tile_cols, FL, TILE), dest_ids, num_segments=NLAT * tile_cols)
    return summed.reshape(NLAT, tile_cols, FL, TILE).transpose(0, 2, 1, 3).reshape(NLAT, FL, NLON)

def spectral_full(block_coeff, wave_ids, local_rates, sine_lat, cos_lat, lat_weight):
    weighted = block_coeff * lat_weight[:, None, None, None]
    order_f = wave_ids.astype(jnp.float32)[:, None]
    diagonal = legendre_diagonal(order_f, cos_lat)
    wave_count = wave_ids.shape[0]
    lat_count = sine_lat.shape[0]
    recurrence = (jnp.zeros((wave_count, lat_count), jnp.float32), jnp.zeros((wave_count, lat_count), jnp.float32), jnp.ones((wave_count, 1), jnp.float32))
    block_size = math.gcd(NM, 128)
    summed = jnp.zeros(block_coeff.shape, jnp.float32)
    for first_degree in range(0, NM, block_size):
        recurrence, legendre = legendre_scan(recurrence, first_degree, block_size, wave_ids, order_f, sine_lat, diagonal)
        degrees = first_degree + jnp.arange(block_size, dtype=jnp.int32)
        spectrum = jnp.einsum('nml,lfcm->fcmn', legendre, weighted, precision=highest)
        damped = spectrum * damping(local_rates, degrees)[:, None, None, :]
        summed = summed + jnp.einsum('nml,fcmn->lfcm', legendre, damped, precision=highest)
    return summed

def reference(adjoint_grid, tile_owner, tile_slot, stencil, interp_weight, vertical_offset, diffusion_rate):
    departed = lagrangian_adjoint(adjoint_grid, tile_owner, tile_slot, stencil, interp_weight)
    diffused = vertical_mix(departed, vertical_offset)
    fourier, wave_ids = fourier_table(NLON, NM, N_LAT)
    coefficients = jnp.einsum('rfx,xc->rfc', diffused, fourier, precision=highest) / NLON
    blocked = coefficients.reshape(NLAT, FL, N_LAT, 2, M_DEV).transpose(2, 0, 1, 3, 4)
    sine_lat, cos_lat = latitude_rows(NLAT, NLAT)
    lat_weight = math.pi / NLAT * cos_lat
    block_ids = jnp.arange(N_LAT, dtype=jnp.int32)

    def one_block(packed):
        block_waves = packed[1] * M_DEV + jnp.arange(M_DEV, dtype=jnp.int32)
        return spectral_full(packed[0], block_waves, diffusion_rate, sine_lat, cos_lat, lat_weight)
    backward = lax.map(one_block, (blocked, block_ids))
    factor = jnp.where(wave_ids == 0, 1.0, 2.0)
    synthesis = backward.transpose(1, 2, 0, 3, 4).reshape(NLAT, FL, 2 * NM) * factor[None, None, :]
    regridded = jnp.einsum('rfc,xc->rfx', synthesis, fourier, precision=highest)
    return diffused + regridded
```

```python
import math

import jax
import jax.numpy as jnp
import ml_dtypes
import numpy as np
from jax import lax
from jax.experimental import pallas as pl
from jax.experimental.pallas import tpu as pltpu
from jax.sharding import PartitionSpec as P

NLAT = 1280
NLON = 3072
NM = 640
FL = 8
STEN = 4
TILE = 128
ROWS = 80
TPR = 3
TILES = 240
N_LAT = 16
N_LON = 8
HALF = NLAT // 2
BAND = NLON // N_LON
GROUPS = 5
WAVE_DEV = 2 * GROUPS
DENSE = N_LON * TPR * ROWS
CHAINS = 4
DEG_PAD = (384, 256, 256, 128, 128)
DEG_USED = (320, 256, 192, 128, 64)
DEG_BASE = (0, 768, 1280, 1792, 2048)
DEG_TOTAL = 2304
VMEM = 60 * 1024 * 1024

f32 = jnp.float32
bf16 = jnp.bfloat16
NT = (((1,), (1,)), ((), ()))
NN = (((1,), (0,)), ((), ()))


def two_parts(values):
    high = values.astype(ml_dtypes.bfloat16)
    low = (values - high.astype(np.float64)).astype(ml_dtypes.bfloat16)
    return high, low


def wave_tables():
    h = np.arange(N_LAT)[:, None]
    g = np.arange(GROUPS)[None, :]
    points = np.arange(BAND)

    def angle(m1):
        waves = (m1 + 8 * h + 128 * g).reshape(-1)
        return (waves[:, None] * points[None, :] % NLON) * (2.0 * math.pi / NLON)

    def rows(first, second):
        return np.stack([first, second], axis=1).reshape(-1, first.shape[-1])

    real = np.stack([rows(np.cos(angle(m1)), -np.sin(angle(m1))) for m1 in (0, 4)])
    mixed = []
    for q in (1, 2, 3):
        a, b = angle(q), angle(8 - q)
        upper = rows(
            np.concatenate([np.cos(a), np.sin(a)], 1), np.concatenate([-np.sin(a), np.cos(a)], 1)
        )
        lower = rows(
            np.concatenate([np.cos(b), -np.sin(b)], 1),
            np.concatenate([-np.sin(b), -np.cos(b)], 1),
        )
        mixed.append(np.concatenate([upper, lower], 0))
    return real, np.stack(mixed)


def log_norms():
    return np.array(
        [
            0.5 * (math.lgamma(m + 1.5) - math.lgamma(m + 1.0) - 0.5 * math.log(math.pi))
            for m in range(NM)
        ]
    )


def split(values):
    high = values.astype(bf16)
    low = (values - high.astype(f32)).astype(bf16)
    return high, low


def dot(a, b, dims):
    return lax.dot_general(a, b, dims, preferred_element_type=f32)


def spread_kernel(grid_ref, stencil_ref, weight_ref, out_ref):
    block = grid_ref.shape[0]
    step = pl.program_id(0)
    target = lax.broadcasted_iota(jnp.int32, (TILE, STEN * TILE), 0).astype(jnp.int16)
    one = jnp.ones((TILE, STEN * TILE), bf16)
    zero = jnp.zeros((TILE, STEN * TILE), bf16)
    for r in range(block):
        for k in range(TPR):
            field = grid_ref[r, :, k * TILE : (k + 1) * TILE]
            scaled = jnp.concatenate(
                [field * weight_ref[r, k, s : s + 1, :] for s in range(STEN)], axis=1
            )
            high = scaled.astype(bf16).astype(f32)
            sides = jnp.concatenate([high, scaled - high], axis=0).astype(bf16)
            points = jnp.concatenate(
                [
                    jnp.broadcast_to(stencil_ref[r, k, s : s + 1, :], (16, TILE))
                    for s in range(STEN)
                ],
                axis=1,
            ).astype(jnp.int16)
            points = jnp.concatenate([points] * (TILE // 16), axis=0)
            hot = jnp.where(points == target, one, zero)
            both = dot(sides, hot, NT)
            tile = step * (block * TPR) + r * TPR + k
            out_ref[pl.ds(tile, FL, stride=TILES), :] = both[:FL] + both[FL:]


def spread_call(grid, stencil, weight):
    block = 8
    return pl.pallas_call(
        spread_kernel,
        grid=(ROWS // block,),
        in_specs=[
            pl.BlockSpec((block, FL, BAND), lambda i: (i, 0, 0)),
            pl.BlockSpec((block, TPR, STEN, TILE), lambda i: (i, 0, 0, 0)),
            pl.BlockSpec((block, TPR, STEN, TILE), lambda i: (i, 0, 0, 0)),
        ],
        out_specs=pl.BlockSpec((FL * TILES, TILE), lambda i: (0, 0)),
        out_shape=jax.ShapeDtypeStruct((FL * TILES, TILE), f32),
        compiler_params=pltpu.CompilerParams(vmem_limit_bytes=VMEM),
        name="spread",
    )(grid, stencil, weight)


def table_kernel(order_ref, norm_ref, sine_ref, logcos_ref, high_ref, low_ref, ring):
    order = order_ref[...]
    order_wide = jnp.concatenate([order] * GROUPS, axis=1)
    norm_wide = jnp.concatenate([norm_ref[...]] * GROUPS, axis=1)
    sine = jnp.broadcast_to(sine_ref[...], (8, HALF))
    exponent = norm_wide + order_wide * logcos_ref[...]
    kept = exponent >= -60.0
    diagonal = jnp.where(kept, jnp.exp(jnp.where(kept, exponent, 0.0)), 0.0)
    order_sq = order * order

    def scale_of(degree):
        return jnp.sqrt(
            jnp.maximum(4.0 * degree * degree - 1.0, 1.0)
            / jnp.maximum(degree * degree - order_sq, 1.0)
        )

    def advance(block, carried):
        previous, earlier, scale_prev = carried
        for local in range(32):
            degree = order + (block * 32 + local).astype(f32)
            scale = scale_of(degree)
            ratio = scale / scale_prev
            wide = jnp.concatenate([scale] * GROUPS, axis=1)
            wide_ratio = jnp.concatenate([ratio] * GROUPS, axis=1)
            stepped = (wide * sine) * previous - wide_ratio * earlier
            if local == 0:
                stepped = jnp.where(block == 0, diagonal, stepped)
            slot = (local % 2) * 16 + local // 2
            for v in range(GROUPS):
                at = v * 256 + slot * 8
                ring[at : at + 8, :] = stepped[:, v * TILE : (v + 1) * TILE]
            earlier = previous
            previous = stepped
            scale_prev = scale
        for g in range(GROUPS):

            @pl.when(block * 16 < DEG_USED[g])
            def _():
                for parity in range(2):
                    rows = jnp.concatenate(
                        [
                            ring[pl.ds(v * 256 + parity * 128 + g, 16, stride=8), :]
                            for v in range(GROUPS)
                        ],
                        axis=1,
                    )
                    high, low = split(rows)
                    start = pl.multiple_of(
                        DEG_BASE[g] + parity * DEG_PAD[g] + block * 16, 16
                    )
                    high_ref[pl.ds(start, 16), :] = high
                    low_ref[pl.ds(start, 16), :] = low

        return previous, earlier, scale_prev

    for g in range(GROUPS):
        extra = DEG_PAD[g] - DEG_USED[g]
        if extra:
            for parity in range(2):
                start = DEG_BASE[g] + parity * DEG_PAD[g] + DEG_USED[g]
                high_ref[start : start + extra, :] = jnp.zeros((extra, HALF), bf16)
                low_ref[start : start + extra, :] = jnp.zeros((extra, HALF), bf16)
    blank = jnp.zeros((8, HALF), f32)
    lax.fori_loop(0, NM // 32, advance, (blank, blank, jnp.ones((8, TILE), f32)))


def table_call(order, norm, sine, logcos):
    shape = jax.ShapeDtypeStruct((DEG_TOTAL, HALF), bf16)
    return pl.pallas_call(
        table_kernel,
        out_shape=(shape, shape),
        scratch_shapes=[pltpu.VMEM((GROUPS * 256, TILE), f32)],
        compiler_params=pltpu.CompilerParams(vmem_limit_bytes=VMEM),
        cost_estimate=pl.CostEstimate(
            flops=640 * 5120 * 20, bytes_accessed=6_000_000, transcendentals=640 * 2048
        ),
        name="legendre_table",
    )(order, norm, sine, logcos)


def fourier_kernel(
    key_ref,
    south_ref,
    tiles_ref,
    real_high,
    real_low,
    mixed_high,
    mixed_low,
    dense_ref,
    out_ref,
    *scratch,
):
    sums = scratch[:CHAINS]
    c_high, c_low = scratch[CHAINS:]
    per_chain = N_LON * TILES // CHAINS
    for chain in sums:
        chain[...] = jnp.zeros(chain.shape, f32)

    def scatter(t, _):
        for c, chain in enumerate(sums):
            at = c * per_chain + t
            slot = key_ref[at]
            chain[pl.ds(slot, 1), :] = chain[pl.ds(slot, 1), :] + tiles_ref[pl.ds(at, 1), :]
        return 0

    lax.fori_loop(0, per_chain, scatter, 0, unroll=4)
    south = south_ref[0]
    root = math.sqrt(0.5)
    blank = jnp.zeros((16, NLON), bf16)
    c_high[240:256, :] = blank
    c_low[240:256, :] = blank

    def butterfly(item, _):
        place = item // 5
        chunk = item % 5
        band = jnp.where(south == 1, 2 - place, place)
        row = pl.multiple_of(place * ROWS + chunk * 16, 16)

        def put(column, values):
            high, low = split(values)
            c_high[pl.ds(row, 16), column : column + TILE] = high
            c_low[pl.ds(row, 16), column : column + TILE] = low

        for k in range(TPR):
            d = []
            for b in range(N_LON):
                start = pl.multiple_of(
                    band * DENSE + (b * TPR + k) * ROWS + chunk * 16, 16
                )
                total = sums[0][pl.ds(start, 16), :]
                for chain in sums[1:]:
                    total = total + chain[pl.ds(start, 16), :]
                dense_ref[pl.ds(start, 16), :] = total
                d.append(total)
            s = [d[i] + d[i + 4] for i in range(4)]
            t = [d[i] - d[i + 4] for i in range(4)]
            even, odd = s[0] + s[2], s[1] + s[3]
            minus = (t[1] - t[3]) * root
            plus = (t[1] + t[3]) * root
            at = k * TILE
            put(at, even + odd)
            put(BAND + at, even - odd)
            put(2 * BAND + at, t[0] + minus)
            put(3 * BAND + at, -t[2] - plus)
            put(4 * BAND + at, s[0] - s[2])
            put(5 * BAND + at, s[3] - s[1])
            put(6 * BAND + at, t[0] - minus)
            put(7 * BAND + at, t[2] - plus)
        return 0

    lax.fori_loop(0, 15, butterfly, 0)

    def emit(m1, block):
        for h in range(N_LAT):
            for g in range(GROUPS):
                start = h * WAVE_DEV + 2 * g
                out_ref[h * 8 + m1, g, :, :] = block[start : start + 2, :]

    for i, m1 in enumerate((0, 4)):
        ch = c_high[:, i * BAND : (i + 1) * BAND]
        cl = c_low[:, i * BAND : (i + 1) * BAND]
        wh, wl = real_high[i], real_low[i]
        emit(m1, dot(wh, ch, NT) + (dot(wh, cl, NT) + dot(wl, ch, NT)))
    for q in (1, 2, 3):
        ch = c_high[:, 2 * q * BAND : (2 * q + 2) * BAND]
        cl = c_low[:, 2 * q * BAND : (2 * q + 2) * BAND]
        for half, m1 in enumerate((q, 8 - q)):
            wh = mixed_high[q - 1, half * 160 : half * 160 + 160, :]
            wl = mixed_low[q - 1, half * 160 : half * 160 + 160, :]
            emit(m1, dot(wh, ch, NT) + (dot(wh, cl, NT) + dot(wl, ch, NT)))


def fourier_call(keys, south, tiles, tables):
    vmem = pl.BlockSpec(memory_space=pltpu.VMEM)
    smem = pl.BlockSpec(memory_space=pltpu.SMEM)
    return pl.pallas_call(
        fourier_kernel,
        in_specs=[smem, smem] + [vmem] * 5,
        out_specs=(vmem, vmem),
        out_shape=(
            jax.ShapeDtypeStruct((3 * DENSE, TILE), f32),
            jax.ShapeDtypeStruct((N_LAT * N_LON, GROUPS, 2, 256), f32),
        ),
        scratch_shapes=[pltpu.VMEM((3 * DENSE, TILE), f32)] * CHAINS
        + [pltpu.VMEM((256, NLON), bf16)] * 2,
        compiler_params=pltpu.CompilerParams(vmem_limit_bytes=VMEM),
        name="scatter_fourier",
    )(keys, south, tiles, *tables)


def legendre_kernel(
    wave_ref, coeff_ref, high_ref, low_ref, mix_ref, weight_ref, rate_ref, out_ref, north, south
):
    weight = weight_ref[...]
    row16 = lax.broadcasted_iota(jnp.int32, (16, HALF), 0)
    first_level = (row16 // 2) % 2 == 0
    dn, xn, ds, xs = (mix_ref[i] for i in range(4))

    def mixed(values, own, cross):
        ahead = pltpu.roll(values, 14, 0)
        behind = pltpu.roll(values, 2, 0)
        other = jnp.where(first_level, ahead, behind)
        return values + own * values + cross * other

    pad = jnp.zeros((16, TILE), f32)
    for g in range(GROUPS):
        north[...] = jnp.zeros(north.shape, f32)
        south[...] = jnp.zeros(south.shape, f32)
        for a in range(N_LAT):
            total, place = (north, a) if a < 8 else (south, 15 - a)
            piece = jnp.concatenate([coeff_ref[a * 8 + f, g, :, :] for f in range(FL)], axis=0)
            piece = jnp.concatenate([piece, pad], axis=1)
            offset = ROWS * place + 48
            base = offset // TILE * TILE
            total[:, base : base + 384] += pltpu.roll(piece, offset % TILE, 1)
        extra_n = north[:, 768:896]
        extra_s = south[:, 768:896]
        north[:, 640:768] += pltpu.roll(extra_s, 48, 1)
        south[:, 640:768] += pltpu.roll(extra_n, 48, 1)
        full_n = mixed(north[:, 128:768], dn, xn)
        full_s = mixed(south[:, 128:768], ds, xs)
        pad_len = DEG_PAD[g]
        wave = wave_ref[0] + 128 * g
        factor = jnp.where(wave == 0, 1.0, 2.0).astype(f32)
        lane = lax.broadcasted_iota(jnp.int32, (16, pad_len), 1)
        rate = jnp.concatenate([rate_ref[...]] * (pad_len // TILE), axis=1)
        results = []
        for parity, folded in enumerate((full_n + full_s, full_n - full_s)):
            folded = folded * weight
            fh, fl = split(folded)
            start = DEG_BASE[g] + parity * pad_len
            ph = high_ref[start : start + pad_len, :]
            pw = low_ref[start : start + pad_len, :]
            spectrum = dot(fh, ph, NT) + (dot(fl, ph, NT) + dot(fh, pw, NT))
            degree = wave + parity + 2 * lane
            degree_f = degree.astype(f32)
            ratio = rate * (degree_f * (degree_f + 1.0) / float(NM * (NM + 1)))
            damped = spectrum * (-ratio / (1.0 + ratio)) * factor
            damped = jnp.where(degree < NM, damped, 0.0)
            dh, dl = split(damped)
            results.append(dot(dh, ph, NN) + (dot(dl, ph, NN) + dot(dh, pw, NN)))
        for a in range(N_LAT):
            place = a if a < 8 else 15 - a
            offset = ROWS * place
            base = offset // TILE * TILE
            shift = offset % TILE
            width = TILE if shift <= 48 else 256
            even = results[0][:, base : base + width]
            odd = results[1][:, base : base + width]
            piece = even + odd if a < 8 else even - odd
            if shift:
                piece = pltpu.roll(piece, width - shift, 1)
            for f in range(FL):
                out_ref[a * 8 + f, g, :, :] = piece[2 * f : 2 * f + 2, :TILE]


def legendre_call(wave, coeff, high, low, mix, weight, rate):
    vmem = pl.BlockSpec(memory_space=pltpu.VMEM)
    smem = pl.BlockSpec(memory_space=pltpu.SMEM)
    return pl.pallas_call(
        legendre_kernel,
        in_specs=[smem] + [vmem] * 6,
        out_specs=vmem,
        out_shape=jax.ShapeDtypeStruct((N_LAT * N_LON, GROUPS, 2, TILE), f32),
        scratch_shapes=[pltpu.VMEM((16, 896), f32)] * 2,
        compiler_params=pltpu.CompilerParams(vmem_limit_bytes=VMEM),
        name="legendre",
    )(wave, coeff, high, low, mix, weight, rate)


def inverse_kernel(
    back_ref,
    real_high,
    real_low,
    mixed_high,
    mixed_low,
    own_ref,
    other_ref,
    mix_ref,
    out_ref,
    waves,
    synth,
):
    for m1 in range(8):
        for h in range(N_LAT):
            for g in range(GROUPS):
                start = m1 * 160 + h * WAVE_DEV + 2 * g
                waves[start : start + 2, :] = back_ref[h * 8 + m1, g, :, :]

    def transform(parts, wh, wl):
        stacked = jnp.concatenate([waves[m1 * 160 : m1 * 160 + 160, :] for m1 in parts], axis=0)
        ah, al = split(stacked.T[:ROWS, :])
        return dot(ah, wh, NN) + (dot(al, wh, NN) + dot(ah, wl, NN))

    for i, m1 in enumerate((0, 4)):
        synth[:, i * BAND : (i + 1) * BAND] = transform((m1,), real_high[i], real_low[i])
    for q in (1, 2, 3):
        synth[:, 2 * q * BAND : (2 * q + 2) * BAND] = transform(
            (q, 8 - q), mixed_high[q - 1], mixed_low[q - 1]
        )
    root = math.sqrt(0.5)

    def combine(chunk, _):
        row = pl.multiple_of(chunk * 16, 16)
        diag = mix_ref[0, pl.ds(row, 16), :]
        cross = mix_ref[1, pl.ds(row, 16), :]
        for k in range(TPR):
            y = [
                synth[pl.ds(row, 16), i * BAND + k * TILE : i * BAND + (k + 1) * TILE]
                for i in range(8)
            ]
            e0, e1 = y[0] + y[1], y[0] - y[1]
            r1, i1, r2, i2, r3, i3 = y[2:]
            even = (e0 + r2, e1 - i2, e0 - r2, e1 + i2)
            odd = (
                r1 + r3,
                ((r1 - i1) - (r3 + i3)) * root,
                i3 - i1,
                ((r3 - i3) - (r1 + i1)) * root,
            )
            for b in range(N_LON):
                at = pl.multiple_of((b * TPR + k) * ROWS + chunk * 16, 16)
                own = own_ref[pl.ds(at, 16), :]
                diffused = own + diag * own + cross * other_ref[pl.ds(at, 16), :]
                wave = even[b % 4] + odd[b % 4] if b < 4 else even[b % 4] - odd[b % 4]
                out_ref[pl.ds(at, 16), :] = diffused + wave
        return 0

    lax.fori_loop(0, ROWS // 16, combine, 0)


def inverse_call(back, tables, own, other, mix):
    vmem = pl.BlockSpec(memory_space=pltpu.VMEM)
    return pl.pallas_call(
        inverse_kernel,
        in_specs=[vmem] * 8,
        out_specs=vmem,
        out_shape=jax.ShapeDtypeStruct((DENSE, TILE), f32),
        scratch_shapes=[pltpu.VMEM((8 * 160, TILE), f32), pltpu.VMEM((ROWS, NLON), f32)],
        compiler_params=pltpu.CompilerParams(vmem_limit_bytes=VMEM),
        name="inverse_fourier",
    )(back, *tables, own, other, mix)


def place_kernel(south_ref, rows_ref, out_ref):
    south = south_ref[0]

    def place(i, _):
        target = jnp.where(south == 1, ROWS - 1 - i, i)
        for k in range(TPR):
            out_ref[target, :, k * TILE : (k + 1) * TILE] = rows_ref[
                pl.ds(k * ROWS + i, FL, stride=TILES), :
            ]
        return 0

    lax.fori_loop(0, ROWS, place, 0, unroll=8)


def place_call(south, rows):
    vmem = pl.BlockSpec(memory_space=pltpu.VMEM)
    smem = pl.BlockSpec(memory_space=pltpu.SMEM)
    return pl.pallas_call(
        place_kernel,
        in_specs=[smem, vmem],
        out_specs=vmem,
        out_shape=jax.ShapeDtypeStruct((ROWS, FL, BAND), f32),
        compiler_params=pltpu.CompilerParams(vmem_limit_bytes=VMEM),
        name="place_rows",
    )(south, rows)


def local(
    adjoint_grid, tile_owner, tile_slot, stencil, interp_weight, vertical_offset, diffusion_rate
):
    lat_here = lax.axis_index("lat")
    lon_here = lax.axis_index("lon")
    is_south = lat_here >= N_LAT // 2
    south = is_south.astype(jnp.int32).reshape(1)
    wave = (lon_here + 8 * lat_here).astype(jnp.int32)

    owners = tile_owner.reshape(TILES)
    slots = tile_slot.reshape(TILES)
    dest_lat = owners // N_LON
    rows = slots // TPR
    rows = jnp.where(dest_lat >= N_LAT // 2, ROWS - 1 - rows, rows)
    columns = (owners % N_LON) * TPR + slots % TPR
    keys = ((dest_lat - lat_here + 1) * (N_LON * TPR) + columns) * ROWS + rows
    keys = lax.all_gather(keys, "lon", tiled=True)

    mix = vertical_offset.reshape(ROWS, 16)
    mix = jnp.where(is_south, jnp.flip(mix, 0), mix).T
    mix_all = lax.all_gather(mix, "lat")
    half = N_LAT // 2
    mix_north = mix_all[:half].transpose(1, 0, 2).reshape(16, HALF)
    mix_south = jnp.flip(mix_all[half:], 0).transpose(1, 0, 2).reshape(16, HALF)
    own_ids = [(f // 2) * 4 + (f % 2) * 2 + f % 2 for f in range(FL)]
    cross_ids = [(f // 2) * 4 + (1 - f % 2) * 2 + f % 2 for f in range(FL)]

    def picked(table, ids):
        return jnp.stack([table[i] for i in ids for _ in range(2)], axis=0)

    mix_waves = jnp.stack(
        [
            picked(mix_north, own_ids),
            picked(mix_north, cross_ids),
            picked(mix_south, own_ids),
            picked(mix_south, cross_ids),
        ]
    )
    level = lon_here % 2
    field = lon_here // 2
    own_row = lax.dynamic_index_in_dim(mix, field * 4 + level * 3, 0, False)
    cross_row = lax.dynamic_index_in_dim(mix, field * 4 + (1 - level) * 2 + level, 0, False)
    mix_grid = jnp.broadcast_to(
        jnp.stack([own_row, cross_row])[:, :, None], (2, ROWS, TILE)
    )

    latitude = 0.5 * math.pi - math.pi * (np.arange(HALF) + 0.5) / NLAT
    sine = jnp.asarray(np.sin(latitude)[None, :], f32)
    logcos = jnp.asarray(np.log(np.cos(latitude))[None, :], f32)
    weight = jnp.asarray((math.pi / NLAT * np.cos(latitude) / NLON)[None, :], f32)
    groups = np.zeros((TILE, 8))
    groups[:, :GROUPS] = log_norms().reshape(GROUPS, TILE).T
    norm = lax.dynamic_index_in_dim(jnp.asarray(groups, f32), wave, 0, False)
    norm = jnp.broadcast_to(norm[:, None], (8, TILE))
    group_start = jnp.minimum(jnp.arange(8, dtype=jnp.int32), GROUPS - 1) * TILE
    order = jnp.broadcast_to((wave + group_start).astype(f32)[:, None], (8, TILE))
    rate = jnp.broadcast_to(
        jnp.repeat(diffusion_rate, 2, total_repeat_length=16)[:, None], (16, TILE)
    )
    real, mixed = wave_tables()
    tables = tuple(jnp.asarray(part) for part in two_parts(real) + two_parts(mixed))

    spread = spread_call(adjoint_grid, stencil, interp_weight)
    tiles = lax.all_to_all(spread, "lon", 0, 0, tiled=True)
    high, low = table_call(order, norm, sine, logcos)
    dense, coeff = fourier_call(keys, south, tiles, tables)
    dense = dense.reshape(3, DENSE, TILE)
    below = lax.ppermute(dense[0], "lat", [(i + 1, i) for i in range(N_LAT - 1)])
    above = lax.ppermute(dense[2], "lat", [(i, i + 1) for i in range(N_LAT - 1)])
    coeff = lax.all_to_all(coeff, ("lat", "lon"), 0, 0, tiled=True)
    back = legendre_call(wave.reshape(1), coeff, high, low, mix_waves, weight, rate)
    departed = dense[1] + below + above
    other = lax.ppermute(departed, "lon", [(i, i ^ 1) for i in range(N_LON)])
    back = lax.all_to_all(back, ("lat", "lon"), 0, 0, tiled=True)
    result = inverse_call(back, tables, departed, other, mix_grid)
    result = lax.all_to_all(result, "lon", 0, 0, tiled=True)
    return place_call(south, result)


def solution(mesh):
    in_specs = (
        P("lat", None, "lon"),
        P("lat", "lon", None, None),
        P("lat", "lon", None, None),
        P("lat", "lon", None, None),
        P("lat", "lon", None, None),
        P("lat", None, None, None),
        P(),
    )
    out_specs = P("lat", None, "lon")
    return jax.shard_map(local, mesh=mesh, in_specs=in_specs, out_specs=out_specs, check_vma=False)
```

```python
import math

import jax
import jax.numpy as jnp
import ml_dtypes
import numpy as np
from jax import lax
from jax.experimental import pallas as pl
from jax.experimental.pallas import tpu as pltpu
from jax.sharding import PartitionSpec as P

NLAT = 1280
NLON = 3072
NM = 640
FL = 8
STEN = 4
TILE = 128
ROWS = 80
TPR = 3
TILES = 240
N_LAT = 16
N_LON = 8
HALF = NLAT // 2
BAND = NLON // N_LON
GROUPS = 5
WAVE_DEV = 2 * GROUPS
DENSE = N_LON * TPR * ROWS
CHUNK = TILES + 8
CHAINS = 4
DEG_PAD = (384, 256, 256, 128, 128)
DEG_USED = (320, 256, 192, 128, 64)
DEG_BASE = (0, 768, 1280, 1792, 2048)
DEG_TOTAL = 2304
VMEM = 60 * 1024 * 1024

f32 = jnp.float32
bf16 = jnp.bfloat16
NT = (((1,), (1,)), ((), ()))
NN = (((1,), (0,)), ((), ()))


def two_parts(values):
    high = values.astype(ml_dtypes.bfloat16)
    low = (values - high.astype(np.float64)).astype(ml_dtypes.bfloat16)
    return high, low


def wave_tables():
    h = np.arange(N_LAT)[:, None]
    g = np.arange(GROUPS)[None, :]
    points = np.arange(BAND)

    def angle(m1):
        waves = (m1 + 8 * h + 128 * g).reshape(-1)
        return (waves[:, None] * points[None, :] % NLON) * (2.0 * math.pi / NLON)

    def rows(first, second):
        return np.stack([first, second], axis=1).reshape(-1, first.shape[-1])

    real = np.stack([rows(np.cos(angle(m1)), -np.sin(angle(m1))) for m1 in (0, 4)])
    mixed = []
    for q in (1, 2, 3):
        a, b = angle(q), angle(8 - q)
        upper = rows(
            np.concatenate([np.cos(a), np.sin(a)], 1), np.concatenate([-np.sin(a), np.cos(a)], 1)
        )
        lower = rows(
            np.concatenate([np.cos(b), -np.sin(b)], 1),
            np.concatenate([-np.sin(b), -np.cos(b)], 1),
        )
        mixed.append(np.concatenate([upper, lower], 0))
    return real, np.stack(mixed)


def log_norms():
    return np.array(
        [
            0.5 * (math.lgamma(m + 1.5) - math.lgamma(m + 1.0) - 0.5 * math.log(math.pi))
            for m in range(NM)
        ]
    )


def split(values):
    high = values.astype(bf16)
    low = (values - high.astype(f32)).astype(bf16)
    return high, low


def stacked_parts(values):
    high = values.astype(bf16).astype(f32)
    return jnp.concatenate([high, values - high], axis=0).astype(bf16)


def dot(a, b, dims):
    return lax.dot_general(a, b, dims, preferred_element_type=f32)


def spread_kernel(lon_ref, grid_ref, stencil_ref, weight_ref, owner_ref, slot_ref, *rest):
    outs, (out_ref, sems) = rest[:N_LON], rest[N_LON:]
    block = grid_ref.shape[0]
    step = pl.program_id(0)
    target = lax.broadcasted_iota(jnp.int32, (TILE, STEN * TILE), 0).astype(jnp.int16)
    one = jnp.ones((TILE, STEN * TILE), bf16)
    zero = jnp.zeros((TILE, STEN * TILE), bf16)
    for r in range(block):
        for k in range(TPR):
            field = grid_ref[r, :, k * TILE : (k + 1) * TILE]
            scaled = jnp.concatenate(
                [field * weight_ref[r, k, s : s + 1, :] for s in range(STEN)], axis=1
            )
            high = scaled.astype(bf16).astype(f32)
            sides = jnp.concatenate([high, scaled - high], axis=0).astype(bf16)
            points = jnp.concatenate(
                [
                    jnp.broadcast_to(stencil_ref[r, k, s : s + 1, :], (16, TILE))
                    for s in range(STEN)
                ],
                axis=1,
            ).astype(jnp.int16)
            points = jnp.concatenate([points] * (TILE // 16), axis=0)
            hot = jnp.where(points == target, one, zero)
            both = dot(sides, hot, NT)
            tile = step * (block * TPR) + r * TPR + k
            out_ref[pl.ds(tile, FL, stride=CHUNK), :] = both[:FL] + both[FL:]

    @pl.when(step == pl.num_programs(0) - 1)
    def _():
        owner, slot = owner_ref[...], slot_ref[...]
        dest_lat = owner // N_LON
        line = (slot * 171) // 512
        column = (owner - dest_lat * N_LON) * TPR + slot - line * TPR
        line = jnp.where(dest_lat >= N_LAT // 2, ROWS - 1 - line, line)
        keys = ((dest_lat - lon_ref[1] + 1) * (N_LON * TPR) + column) * ROWS + line
        keys = keys.astype(f32)
        for f in range(FL):
            at = f * CHUNK + TILES
            out_ref[at : at + 8, :] = jnp.zeros((8, TILE), f32)
            out_ref[at : at + 1, :] = keys[:, :TILE]
            out_ref[at + 1 : at + 2, : TILES - TILE] = keys[:, TILE:]
        exchange = [
            pltpu.make_async_copy(
                out_ref.at[pl.ds(pl.multiple_of((lon_ref[0] ^ k) * CHUNK, 8), CHUNK), :],
                outs[k],
                sems.at[k],
            )
            for k in range(N_LON)
        ]
        for copy in exchange:
            copy.start()
        for copy in exchange:
            copy.wait()


def spread_call(lon, grid, stencil, weight, owner, slot):
    block = 8
    return pl.pallas_call(
        spread_kernel,
        grid=(ROWS // block,),
        in_specs=[
            pl.BlockSpec(memory_space=pltpu.SMEM),
            pl.BlockSpec((block, FL, BAND), lambda i: (i, 0, 0)),
            pl.BlockSpec((block, TPR, STEN, TILE), lambda i: (i, 0, 0, 0)),
            pl.BlockSpec((block, TPR, STEN, TILE), lambda i: (i, 0, 0, 0)),
            pl.BlockSpec((1, TILES), lambda i: (0, 0)),
            pl.BlockSpec((1, TILES), lambda i: (0, 0)),
        ],
        out_specs=[pl.BlockSpec(memory_space=pl.ANY)] * N_LON,
        out_shape=[jax.ShapeDtypeStruct((CHUNK, TILE), f32)] * N_LON,
        scratch_shapes=[
            pltpu.VMEM((FL * CHUNK, TILE), f32),
            pltpu.SemaphoreType.DMA((N_LON,)),
        ],
        compiler_params=pltpu.CompilerParams(vmem_limit_bytes=VMEM),
        name="spread",
    )(lon, grid, stencil, weight, owner, slot)


def table_kernel(order_ref, norm_ref, sine_ref, logcos_ref, high_ref, low_ref, ring):
    order = order_ref[...]
    order_wide = jnp.concatenate([order] * GROUPS, axis=1)
    norm_wide = jnp.concatenate([norm_ref[...]] * GROUPS, axis=1)
    sine = jnp.broadcast_to(sine_ref[...], (8, HALF))
    exponent = norm_wide + order_wide * logcos_ref[...]
    kept = exponent >= -60.0
    diagonal = jnp.where(kept, jnp.exp(jnp.where(kept, exponent, 0.0)), 0.0)
    order_sq = order * order

    def scale_of(degree):
        return jnp.sqrt(
            jnp.maximum(4.0 * degree * degree - 1.0, 1.0)
            / jnp.maximum(degree * degree - order_sq, 1.0)
        )

    def advance(block, carried):
        previous, earlier, scale_prev = carried
        for local in range(32):
            degree = order + (block * 32 + local).astype(f32)
            scale = scale_of(degree)
            ratio = scale / scale_prev
            wide = jnp.concatenate([scale] * GROUPS, axis=1)
            wide_ratio = jnp.concatenate([ratio] * GROUPS, axis=1)
            stepped = (wide * sine) * previous - wide_ratio * earlier
            if local == 0:
                stepped = jnp.where(block == 0, diagonal, stepped)
            slot = (local % 2) * 16 + local // 2
            for v in range(GROUPS):
                at = v * 256 + slot * 8
                ring[at : at + 8, :] = stepped[:, v * TILE : (v + 1) * TILE]
            earlier = previous
            previous = stepped
            scale_prev = scale
        for g in range(GROUPS):

            @pl.when(block * 16 < DEG_USED[g])
            def _():
                for parity in range(2):
                    rows = jnp.concatenate(
                        [
                            ring[pl.ds(v * 256 + parity * 128 + g, 16, stride=8), :]
                            for v in range(GROUPS)
                        ],
                        axis=1,
                    )
                    high, low = split(rows)
                    start = pl.multiple_of(
                        DEG_BASE[g] + parity * DEG_PAD[g] + block * 16, 16
                    )
                    high_ref[pl.ds(start, 16), :] = high
                    low_ref[pl.ds(start, 16), :] = low

        return previous, earlier, scale_prev

    for g in range(GROUPS):
        extra = DEG_PAD[g] - DEG_USED[g]
        if extra:
            for parity in range(2):
                start = DEG_BASE[g] + parity * DEG_PAD[g] + DEG_USED[g]
                high_ref[start : start + extra, :] = jnp.zeros((extra, HALF), bf16)
                low_ref[start : start + extra, :] = jnp.zeros((extra, HALF), bf16)
    blank = jnp.zeros((8, HALF), f32)
    lax.fori_loop(0, NM // 32, advance, (blank, blank, jnp.ones((8, TILE), f32)))


def table_call(order, norm, sine, logcos):
    shape = jax.ShapeDtypeStruct((DEG_TOTAL, HALF), bf16)
    return pl.pallas_call(
        table_kernel,
        out_shape=(shape, shape),
        scratch_shapes=[pltpu.VMEM((GROUPS * 256, TILE), f32)],
        compiler_params=pltpu.CompilerParams(vmem_limit_bytes=VMEM),
        cost_estimate=pl.CostEstimate(
            flops=640 * 5120 * 20, bytes_accessed=6_000_000, transcendentals=640 * 2048
        ),
        name="legendre_table",
    )(order, norm, sine, logcos)


def fourier_kernel(south_ref, *refs):
    chunks = refs[:N_LON]
    real_high, real_low, mixed_high, mixed_low, extra_ref = refs[N_LON : N_LON + 5]
    bands = refs[N_LON + 5 : N_LON + 8]
    out_ref = refs[N_LON + 8]
    scratch = refs[N_LON + 9 :]
    sums = scratch[:CHAINS]
    c_high, c_low, tiles, keys, dense_ref, sems = scratch[CHAINS:]
    loads = []
    for k in range(N_LON):
        loads.append(pltpu.make_async_copy(chunks[k], tiles.at[k], sems.at[k]))
        loads.append(
            pltpu.make_async_copy(
                chunks[k].at[pl.ds(TILES, 8), :], keys.at[k], sems.at[N_LON + k]
            )
        )
    for copy in loads:
        copy.start()
    for chain in sums:
        chain[...] = jnp.zeros(chain.shape, f32)
    for copy in loads:
        copy.wait()
    share = N_LON // CHAINS
    for part in range(share):
        for line, count in ((0, TILE), (1, TILES - TILE)):

            def scatter(t, _):
                for c, chain in enumerate(sums):
                    k = c * share + part
                    slot = keys[k, line, t].astype(jnp.int32)
                    tile = tiles[k, pl.ds(line * TILE + t, 1), :]
                    chain[pl.ds(slot, 1), :] = chain[pl.ds(slot, 1), :] + tile
                return 0

            lax.fori_loop(0, count, scatter, 0, unroll=4)
    south = south_ref[0]
    root = math.sqrt(0.5)
    blank = jnp.zeros((16, NLON), bf16)
    c_high[240:256, :] = blank
    c_low[240:256, :] = blank

    def butterfly(item, _):
        place = item // 5
        chunk = item % 5
        band = jnp.where(south == 1, 2 - place, place)
        row = pl.multiple_of(place * ROWS + chunk * 16, 16)

        def put(column, values):
            high, low = split(values)
            c_high[pl.ds(row, 16), column : column + TILE] = high
            c_low[pl.ds(row, 16), column : column + TILE] = low

        for k in range(TPR):
            d = []
            for b in range(N_LON):
                start = pl.multiple_of(
                    band * DENSE + (b * TPR + k) * ROWS + chunk * 16, 16
                )
                total = sums[0][pl.ds(start, 16), :]
                for chain in sums[1:]:
                    total = total + chain[pl.ds(start, 16), :]
                dense_ref[pl.ds(start, 16), :] = total
                d.append(total)
            s = [d[i] + d[i + 4] for i in range(4)]
            t = [d[i] - d[i + 4] for i in range(4)]
            even, odd = s[0] + s[2], s[1] + s[3]
            minus = (t[1] - t[3]) * root
            plus = (t[1] + t[3]) * root
            at = k * TILE
            put(at, even + odd)
            put(BAND + at, even - odd)
            put(2 * BAND + at, t[0] + minus)
            put(3 * BAND + at, -t[2] - plus)
            put(4 * BAND + at, s[0] - s[2])
            put(5 * BAND + at, s[3] - s[1])
            put(6 * BAND + at, t[0] - minus)
            put(7 * BAND + at, t[2] - plus)
        return 0

    lax.fori_loop(0, 15, butterfly, 0)
    stores = [
        pltpu.make_async_copy(
            dense_ref.at[pl.ds(i * DENSE, DENSE), :], bands[i], sems.at[2 * N_LON + i]
        )
        for i in range(3)
    ]
    for copy in stores:
        copy.start()
    extra = extra_ref[...]

    def emit(m1, block):
        block = jnp.concatenate([block[:, :TILE], block[:, TILE:] + extra], axis=1)
        for h in range(N_LAT):
            for g in range(GROUPS):
                start = h * WAVE_DEV + 2 * g
                out_ref[h * 8 + m1, g, :, :] = block[start : start + 2, :]

    def transform(ch, cl, wh, wl):
        rows = wh.shape[0]
        both = dot(jnp.concatenate([wh, wl], axis=0), ch, NT)
        return both[:rows] + (both[rows:] + dot(wh, cl, NT))

    for i, m1 in enumerate((0, 4)):
        at = slice(i * BAND, (i + 1) * BAND)
        emit(m1, transform(c_high[:, at], c_low[:, at], real_high[i], real_low[i]))
    for q in (1, 2, 3):
        at = slice(2 * q * BAND, (2 * q + 2) * BAND)
        pair = transform(c_high[:, at], c_low[:, at], mixed_high[q - 1], mixed_low[q - 1])
        emit(q, pair[:160])
        emit(8 - q, pair[160:])
    for copy in stores:
        copy.wait()


def fourier_call(south, chunks, tables, extra):
    vmem = pl.BlockSpec(memory_space=pltpu.VMEM)
    smem = pl.BlockSpec(memory_space=pltpu.SMEM)
    return pl.pallas_call(
        fourier_kernel,
        in_specs=[smem] + [pl.BlockSpec(memory_space=pl.ANY)] * N_LON + [vmem] * 5,
        out_specs=[pl.BlockSpec(memory_space=pl.ANY)] * 3 + [vmem],
        out_shape=[jax.ShapeDtypeStruct((DENSE, TILE), f32)] * 3
        + [jax.ShapeDtypeStruct((N_LAT * N_LON, GROUPS, 2, 256), f32)],
        scratch_shapes=[pltpu.VMEM((3 * DENSE, TILE), f32)] * CHAINS
        + [pltpu.VMEM((256, NLON), bf16)] * 2
        + [
            pltpu.VMEM((N_LON, CHUNK, TILE), f32),
            pltpu.SMEM((N_LON, 8, TILE), f32),
            pltpu.VMEM((3 * DENSE, TILE), f32),
            pltpu.SemaphoreType.DMA((2 * N_LON + 3,)),
        ],
        compiler_params=pltpu.CompilerParams(vmem_limit_bytes=VMEM),
        name="scatter_fourier",
    )(south, *chunks, *tables, extra)


def legendre_kernel(
    wave_ref, coeff_ref, high_ref, low_ref, weight_ref, rate_ref, out_ref, north, south, blend
):
    weight = weight_ref[...]
    row16 = lax.broadcasted_iota(jnp.int32, (16, HALF), 0)
    first_level = (row16 // 2) % 2 == 0
    is_first = row16 % 2 == 0
    lane128 = lax.broadcasted_iota(jnp.int32, (16, TILE), 1)
    is_blend = lane128 >= TILE - 16

    def mixed(values, own, cross):
        ahead = pltpu.roll(values, 14, 0)
        behind = pltpu.roll(values, 2, 0)
        other = jnp.where(first_level, ahead, behind)
        return values + own * values + cross * other

    pad = jnp.zeros((16, TILE), f32)
    north[...] = jnp.zeros(north.shape, f32)
    south[...] = jnp.zeros(south.shape, f32)
    blend[...] = jnp.zeros(blend.shape, f32)
    for g in range(GROUPS):
        for a in range(N_LAT):
            total, place = (north, a) if a < 8 else (south, 15 - a)
            piece = jnp.concatenate([coeff_ref[a * 8 + f, g, :, :] for f in range(FL)], axis=0)
            last = piece[:, TILE:]
            piece = jnp.concatenate([piece[:, :TILE], jnp.where(is_blend, 0.0, last), pad], axis=1)
            offset = ROWS * place + 48
            base = offset // TILE * TILE
            total[g, :, base : base + 384] += pltpu.roll(piece, offset % TILE, 1)
            offset = ROWS * place + 16 * g
            base = offset // TILE * TILE
            last = pltpu.roll(jnp.where(is_blend, last, 0.0), (offset % TILE + 16) % TILE, 1)
            blend[a // 8, :, base : base + TILE] += last
    blends = []
    for side in range(2):
        both = blend[side]
        blends.append(jnp.where(is_first, both, pltpu.roll(both, 1, 0)))
        blends.append(jnp.where(is_first, pltpu.roll(both, 15, 0), both))
    dn, xn, ds, xs = blends
    for g in range(GROUPS):
        extra_n = north[g, :, 768:896]
        extra_s = south[g, :, 768:896]
        north[g, :, 640:768] += pltpu.roll(extra_s, 48, 1)
        south[g, :, 640:768] += pltpu.roll(extra_n, 48, 1)
        full_n = mixed(north[g, :, 128:768], dn, xn)
        full_s = mixed(south[g, :, 128:768], ds, xs)
        pad_len = DEG_PAD[g]
        wave = wave_ref[0] + 128 * g
        factor = jnp.where(wave == 0, 1.0, 2.0).astype(f32)
        lane = lax.broadcasted_iota(jnp.int32, (16, pad_len), 1)
        rate = jnp.concatenate([rate_ref[...]] * (pad_len // TILE), axis=1)
        results = []
        for parity, folded in enumerate((full_n + full_s, full_n - full_s)):
            folded = folded * weight
            both = stacked_parts(folded)
            start = DEG_BASE[g] + parity * pad_len
            ph = high_ref[start : start + pad_len, :]
            pw = low_ref[start : start + pad_len, :]
            main = dot(both, ph, NT)
            spectrum = main[:16] + (main[16:] + dot(both[:16], pw, NT))
            degree = wave + parity + 2 * lane
            degree_f = degree.astype(f32)
            ratio = rate * (degree_f * (degree_f + 1.0) / float(NM * (NM + 1)))
            damped = spectrum * (-ratio / (1.0 + ratio)) * factor
            damped = jnp.where(degree < NM, damped, 0.0)
            both = stacked_parts(damped)
            main = dot(both, ph, NN)
            results.append(main[:16] + (main[16:] + dot(both[:16], pw, NN)))
        for a in range(N_LAT):
            place = a if a < 8 else 15 - a
            offset = ROWS * place
            base = offset // TILE * TILE
            shift = offset % TILE
            width = TILE if shift <= 48 else 256
            even = results[0][:, base : base + width]
            odd = results[1][:, base : base + width]
            piece = even + odd if a < 8 else even - odd
            if shift:
                piece = pltpu.roll(piece, width - shift, 1)
            for f in range(FL):
                out_ref[a * 8 + f, g, :, :] = piece[2 * f : 2 * f + 2, :TILE]


def legendre_call(wave, coeff, high, low, weight, rate):
    vmem = pl.BlockSpec(memory_space=pltpu.VMEM)
    smem = pl.BlockSpec(memory_space=pltpu.SMEM)
    return pl.pallas_call(
        legendre_kernel,
        in_specs=[smem] + [vmem] * 5,
        out_specs=vmem,
        out_shape=jax.ShapeDtypeStruct((N_LAT * N_LON, GROUPS, 2, TILE), f32),
        scratch_shapes=[pltpu.VMEM((GROUPS, 16, 896), f32)] * 2
        + [pltpu.VMEM((2, 16, HALF), f32)],
        compiler_params=pltpu.CompilerParams(vmem_limit_bytes=VMEM),
        name="legendre",
    )(wave, coeff, high, low, weight, rate)


def synthesis_kernel(back_ref, real_high, real_low, mixed_high, mixed_low, synth, waves):
    for m1 in range(8):
        for h in range(N_LAT):
            for g in range(GROUPS):
                start = m1 * 160 + h * WAVE_DEV + 2 * g
                waves[start : start + 2, :] = back_ref[h * 8 + m1, g, :, :]

    def transform(parts, wh, wl):
        stacked = jnp.concatenate([waves[m1 * 160 : m1 * 160 + 160, :] for m1 in parts], axis=0)
        both = stacked_parts(stacked.T[:ROWS, :])
        main = dot(both, wh, NN)
        return main[:ROWS] + (main[ROWS:] + dot(both[:ROWS], wl, NN))

    for i, m1 in enumerate((0, 4)):
        synth[:, i * BAND : (i + 1) * BAND] = transform((m1,), real_high[i], real_low[i])
    for q in (1, 2, 3):
        synth[:, 2 * q * BAND : (2 * q + 2) * BAND] = transform(
            (q, 8 - q), mixed_high[q - 1], mixed_low[q - 1]
        )


def synthesis_call(back, tables):
    vmem = pl.BlockSpec(memory_space=pltpu.VMEM)
    return pl.pallas_call(
        synthesis_kernel,
        in_specs=[vmem] * 5,
        out_specs=vmem,
        out_shape=jax.ShapeDtypeStruct((ROWS, NLON), f32),
        scratch_shapes=[pltpu.VMEM((8 * 160, TILE), f32)],
        compiler_params=pltpu.CompilerParams(vmem_limit_bytes=VMEM),
        cost_estimate=pl.CostEstimate(
            flops=6 * 80 * 860_160, bytes_accessed=8_000_000, transcendentals=0
        ),
        name="wave_synthesis",
    )(back, *tables)


def combine_kernel(lon_ref, synth, own_ref, other_ref, mix_ref, *rest):
    outs, (out_ref, sems) = rest[:N_LON], rest[N_LON:]
    root = math.sqrt(0.5)

    def combine(chunk, _):
        row = pl.multiple_of(chunk * 16, 16)
        diag = mix_ref[0, pl.ds(row, 16), :]
        cross = mix_ref[1, pl.ds(row, 16), :]
        for k in range(TPR):
            y = [
                synth[pl.ds(row, 16), i * BAND + k * TILE : i * BAND + (k + 1) * TILE]
                for i in range(8)
            ]
            e0, e1 = y[0] + y[1], y[0] - y[1]
            r1, i1, r2, i2, r3, i3 = y[2:]
            even = (e0 + r2, e1 - i2, e0 - r2, e1 + i2)
            odd = (
                r1 + r3,
                ((r1 - i1) - (r3 + i3)) * root,
                i3 - i1,
                ((r3 - i3) - (r1 + i1)) * root,
            )
            for b in range(N_LON):
                at = pl.multiple_of((b * TPR + k) * ROWS + chunk * 16, 16)
                own = own_ref[pl.ds(at, 16), :]
                diffused = own + diag * own + cross * other_ref[pl.ds(at, 16), :]
                wave = even[b % 4] + odd[b % 4] if b < 4 else even[b % 4] - odd[b % 4]
                out_ref[pl.ds(at, 16), :] = diffused + wave
        return 0

    lax.fori_loop(0, ROWS // 16, combine, 0)
    exchange = [
        pltpu.make_async_copy(
            out_ref.at[pl.ds(pl.multiple_of((lon_ref[0] ^ k) * TILES, 8), TILES), :],
            outs[k],
            sems.at[k],
        )
        for k in range(N_LON)
    ]
    for copy in exchange:
        copy.start()
    for copy in exchange:
        copy.wait()


def combine_call(lon, synth, own, other, mix):
    vmem = pl.BlockSpec(memory_space=pltpu.VMEM)
    smem = pl.BlockSpec(memory_space=pltpu.SMEM)
    return pl.pallas_call(
        combine_kernel,
        in_specs=[smem] + [vmem] * 4,
        out_specs=[pl.BlockSpec(memory_space=pl.ANY)] * N_LON,
        out_shape=[jax.ShapeDtypeStruct((TILES, TILE), f32)] * N_LON,
        scratch_shapes=[
            pltpu.VMEM((DENSE, TILE), f32),
            pltpu.SemaphoreType.DMA((N_LON,)),
        ],
        compiler_params=pltpu.CompilerParams(vmem_limit_bytes=VMEM),
        name="combine",
    )(lon, synth, own, other, mix)


def place_kernel(south_ref, lon_ref, *rest):
    chunks, (out_ref, rows_ref, sems) = rest[:N_LON], rest[N_LON:]
    south = south_ref[0]
    loads = [
        pltpu.make_async_copy(
            chunks[k],
            rows_ref.at[pl.ds(pl.multiple_of((lon_ref[0] ^ k) * TILES, 8), TILES), :],
            sems.at[k],
        )
        for k in range(N_LON)
    ]
    for copy in loads:
        copy.start()
    for copy in loads:
        copy.wait()

    def place(i, _):
        target = jnp.where(south == 1, ROWS - 1 - i, i)
        for k in range(TPR):
            out_ref[target, :, k * TILE : (k + 1) * TILE] = rows_ref[
                pl.ds(k * ROWS + i, FL, stride=TILES), :
            ]
        return 0

    lax.fori_loop(0, ROWS, place, 0, unroll=8)


def place_call(south, lon, chunks):
    vmem = pl.BlockSpec(memory_space=pltpu.VMEM)
    smem = pl.BlockSpec(memory_space=pltpu.SMEM)
    return pl.pallas_call(
        place_kernel,
        in_specs=[smem, smem] + [pl.BlockSpec(memory_space=pl.ANY)] * N_LON,
        out_specs=vmem,
        out_shape=jax.ShapeDtypeStruct((ROWS, FL, BAND), f32),
        scratch_shapes=[
            pltpu.VMEM((FL * TILES, TILE), f32),
            pltpu.SemaphoreType.DMA((N_LON,)),
        ],
        compiler_params=pltpu.CompilerParams(vmem_limit_bytes=VMEM),
        name="place_rows",
    )(south, lon, *chunks)


def local(
    adjoint_grid, tile_owner, tile_slot, stencil, interp_weight, vertical_offset, diffusion_rate
):
    lat_here = lax.axis_index("lat")
    lon_here = lax.axis_index("lon")
    is_south = lat_here >= N_LAT // 2
    south = is_south.astype(jnp.int32).reshape(1)
    wave = (lon_here + 8 * lat_here).astype(jnp.int32)

    mix = vertical_offset.reshape(ROWS, 16)
    mix = jnp.where(is_south, jnp.flip(mix, 0), mix).T
    level = lon_here % 2
    field = lon_here // 2
    own_row = lax.dynamic_index_in_dim(mix, field * 4 + level * 3, 0, False)
    cross_row = lax.dynamic_index_in_dim(mix, field * 4 + (1 - level) * 2 + level, 0, False)
    blend = jnp.stack([own_row, cross_row])
    mix_grid = jnp.broadcast_to(blend[:, :, None], (2, ROWS, TILE))
    extra = blend.reshape(2, GROUPS, 16).transpose(1, 0, 2).reshape(WAVE_DEV, 16)
    extra = jnp.pad(jnp.tile(extra, (N_LAT, 1)), ((0, 0), (TILE - 16, 0)))

    latitude = 0.5 * math.pi - math.pi * (np.arange(HALF) + 0.5) / NLAT
    sine = jnp.asarray(np.sin(latitude)[None, :], f32)
    logcos = jnp.asarray(np.log(np.cos(latitude))[None, :], f32)
    weight = jnp.asarray((math.pi / NLAT * np.cos(latitude) / NLON)[None, :], f32)
    groups = np.zeros((TILE, 8))
    groups[:, :GROUPS] = log_norms().reshape(GROUPS, TILE).T
    norm = lax.dynamic_index_in_dim(jnp.asarray(groups, f32), wave, 0, False)
    norm = jnp.broadcast_to(norm[:, None], (8, TILE))
    group_start = jnp.minimum(jnp.arange(8, dtype=jnp.int32), GROUPS - 1) * TILE
    order = jnp.broadcast_to((wave + group_start).astype(f32)[:, None], (8, TILE))
    rate = jnp.broadcast_to(
        jnp.repeat(diffusion_rate, 2, total_repeat_length=16)[:, None], (16, TILE)
    )
    real, mixed = wave_tables()
    tables = tuple(jnp.asarray(part) for part in two_parts(real) + two_parts(mixed))

    lon = lon_here.astype(jnp.int32).reshape(1)

    def exchanged(chunks):
        return [chunks[0]] + [
            lax.ppermute(chunks[k], "lon", [(i, i ^ k) for i in range(N_LON)])
            for k in range(1, N_LON)
        ]

    chunks = exchanged(spread_call(
        jnp.stack([lon_here, lat_here]).astype(jnp.int32),
        adjoint_grid,
        stencil,
        interp_weight,
        tile_owner.reshape(1, TILES),
        tile_slot.reshape(1, TILES),
    ))
    high, low = table_call(order, norm, sine, logcos)
    tables, high, low, extra, rate, mix_grid = lax.optimization_barrier(
        (tables, high, low, extra, rate, mix_grid)
    )
    dense_below, dense_here, dense_above, coeff = fourier_call(south, chunks, tables, extra)
    coeff = lax.all_to_all(coeff, ("lat", "lon"), 0, 0, tiled=True)
    dense_below, dense_above, coeff = lax.optimization_barrier((dense_below, dense_above, coeff))
    below = lax.ppermute(dense_below, "lat", [(i + 1, i) for i in range(N_LAT - 1)])
    above = lax.ppermute(dense_above, "lat", [(i, i + 1) for i in range(N_LAT - 1)])
    back = legendre_call(wave.reshape(1), coeff, high, low, weight, rate)
    back = lax.all_to_all(back, ("lat", "lon"), 0, 0, tiled=True)
    dense_here, back = lax.optimization_barrier((dense_here, back))
    departed = dense_here + below + above
    other = lax.ppermute(departed, "lon", [(i, i ^ 1) for i in range(N_LON)])
    synth = synthesis_call(back, tables)
    result = exchanged(combine_call(lon, synth, departed, other, mix_grid))
    return place_call(south, lon, result)


def solution(mesh):
    in_specs = (
        P("lat", None, "lon"),
        P("lat", "lon", None, None),
        P("lat", "lon", None, None),
        P("lat", "lon", None, None),
        P("lat", "lon", None, None),
        P("lat", None, None, None),
        P(),
    )
    out_specs = P("lat", None, "lon")
    return jax.shard_map(local, mesh=mesh, in_specs=in_specs, out_specs=out_specs, check_vma=False)
```

```python
import math

import jax
import jax.numpy as jnp
import ml_dtypes
import numpy as np
from jax import lax
from jax.experimental import pallas as pl
from jax.experimental.pallas import tpu as pltpu
from jax.sharding import PartitionSpec as P

NLAT = 1280
NLON = 3072
NM = 640
FL = 8
STEN = 4
TILE = 128
ROWS = 80
TPR = 3
TILES = 240
N_LAT = 16
N_LON = 8
HALF = NLAT // 2
BAND = NLON // N_LON
GROUPS = 5
WAVE_DEV = 2 * GROUPS
DENSE = N_LON * TPR * ROWS
CHUNK = TILES + 8
CHAINS = 4
DEG_PAD = (384, 256, 256, 128, 128)
DEG_USED = (320, 256, 192, 128, 64)
DEG_BASE = (0, 768, 1280, 1792, 2048)
DEG_TOTAL = 2304
VMEM = 40 * 1024 * 1024
VMEM_LARGE = 60 * 1024 * 1024

f32 = jnp.float32
bf16 = jnp.bfloat16
NT = (((1,), (1,)), ((), ()))
NN = (((1,), (0,)), ((), ()))


def two_parts(values):
    high = values.astype(ml_dtypes.bfloat16)
    low = (values - high.astype(np.float64)).astype(ml_dtypes.bfloat16)
    return high, low


def wave_tables():
    h = np.arange(N_LAT)[:, None]
    g = np.arange(GROUPS)[None, :]
    points = np.arange(BAND)

    def angle(m1):
        waves = (m1 + 8 * h + 128 * g).reshape(-1)
        return (waves[:, None] * points[None, :] % NLON) * (2.0 * math.pi / NLON)

    def rows(first, second):
        return np.stack([first, second], axis=1).reshape(-1, first.shape[-1])

    real = np.stack([rows(np.cos(angle(m1)), -np.sin(angle(m1))) for m1 in (0, 4)])
    mixed = []
    for q in (1, 2, 3):
        a, b = angle(q), angle(8 - q)
        upper = rows(
            np.concatenate([np.cos(a), np.sin(a)], 1), np.concatenate([-np.sin(a), np.cos(a)], 1)
        )
        lower = rows(
            np.concatenate([np.cos(b), -np.sin(b)], 1),
            np.concatenate([-np.sin(b), -np.cos(b)], 1),
        )
        mixed.append(np.concatenate([upper, lower], 0))
    return real, np.stack(mixed)


def log_norms():
    return np.array(
        [
            0.5 * (math.lgamma(m + 1.5) - math.lgamma(m + 1.0) - 0.5 * math.log(math.pi))
            for m in range(NM)
        ]
    )


def first_lanes():
    latitude = 0.5 * math.pi - math.pi * (np.arange(HALF) + 0.5) / NLAT
    exponent = log_norms()[:, None] + np.arange(NM)[:, None] * np.log(np.cos(latitude))[None, :]
    firsts = np.argmax(exponent >= -61.0, axis=1).reshape(GROUPS, NM // GROUPS).min(axis=1)
    return [int(first) // TILE * TILE for first in firsts]


LANES = first_lanes()


def split(values):
    high = values.astype(bf16)
    low = (values - high.astype(f32)).astype(bf16)
    return high, low


def stacked_parts(values):
    high = values.astype(bf16).astype(f32)
    return jnp.concatenate([high, values - high], axis=0).astype(bf16)


def dot(a, b, dims):
    return lax.dot_general(a, b, dims, preferred_element_type=f32)


def spread_kernel(lon_ref, grid_ref, stencil_ref, weight_ref, owner_ref, slot_ref, *rest):
    outs, (out_ref, sems) = rest[:N_LON], rest[N_LON:]
    block = grid_ref.shape[0]
    step = pl.program_id(0)
    target = lax.broadcasted_iota(jnp.int32, (TILE, TILE), 0).astype(jnp.int16)

    def tall(row, kind):
        block16 = jnp.broadcast_to(row, (16, TILE)).astype(kind)
        return jnp.concatenate([block16] * (TILE // 16), axis=0)

    for r in range(block):
        for k in range(TPR):
            field = grid_ref[r, :, k * TILE : (k + 1) * TILE]
            points = [stencil_ref[r, k, s : s + 1, :] for s in range(STEN)]
            weights = [weight_ref[r, k, s : s + 1, :] for s in range(STEN)]
            for s in range(STEN):
                for later in range(s + 1, STEN):
                    weights[s] = weights[s] + jnp.where(
                        points[later] == points[s], weight_ref[r, k, later : later + 1, :], 0.0
                    )
            high = jnp.zeros((TILE, TILE), bf16)
            low = high
            for s in reversed(range(STEN)):
                top = weights[s].astype(bf16).astype(f32)
                here = tall(points[s], jnp.int16) == target
                high = jnp.where(here, tall(top, bf16), high)
                low = jnp.where(here, tall(weights[s] - top, bf16), low)
            top = field.astype(bf16).astype(f32)
            sides = jnp.concatenate(
                [
                    jnp.concatenate([top, field - top], axis=0),
                    jnp.concatenate([top, jnp.zeros_like(top)], axis=0),
                ],
                axis=1,
            ).astype(bf16)
            both = dot(sides, jnp.concatenate([high, low], axis=1), NT)
            tile = step * (block * TPR) + r * TPR + k
            out_ref[pl.ds(tile, FL, stride=CHUNK), :] = both[:FL] + both[FL:]

    @pl.when(step == pl.num_programs(0) - 1)
    def _():
        owner, slot = owner_ref[...], slot_ref[...]
        dest_lat = owner // N_LON
        line = (slot * 171) // 512
        column = (owner - dest_lat * N_LON) * TPR + slot - line * TPR
        line = jnp.where(dest_lat >= N_LAT // 2, ROWS - 1 - line, line)
        keys = ((dest_lat - lon_ref[1] + 1) * (N_LON * TPR) + column) * ROWS + line
        keys = keys.astype(f32)
        for f in range(FL):
            at = f * CHUNK + TILES
            out_ref[at : at + 8, :] = jnp.zeros((8, TILE), f32)
            out_ref[at : at + 1, :] = keys[:, :TILE]
            out_ref[at + 1 : at + 2, : TILES - TILE] = keys[:, TILE:]
        exchange = [
            pltpu.make_async_copy(
                out_ref.at[pl.ds(pl.multiple_of((lon_ref[0] ^ k) * CHUNK, 8), CHUNK), :],
                outs[k],
                sems.at[k],
            )
            for k in range(N_LON)
        ]
        for copy in exchange:
            copy.start()
        for copy in exchange:
            copy.wait()


def spread_call(lon, grid, stencil, weight, owner, slot):
    block = 40
    return pl.pallas_call(
        spread_kernel,
        grid=(ROWS // block,),
        in_specs=[
            pl.BlockSpec(memory_space=pltpu.SMEM),
            pl.BlockSpec((block, FL, BAND), lambda i: (i, 0, 0)),
            pl.BlockSpec((block, TPR, STEN, TILE), lambda i: (i, 0, 0, 0)),
            pl.BlockSpec((block, TPR, STEN, TILE), lambda i: (i, 0, 0, 0)),
            pl.BlockSpec((1, TILES), lambda i: (0, 0)),
            pl.BlockSpec((1, TILES), lambda i: (0, 0)),
        ],
        out_specs=[pl.BlockSpec(memory_space=pl.ANY)] * N_LON,
        out_shape=[jax.ShapeDtypeStruct((CHUNK, TILE), f32)] * N_LON,
        scratch_shapes=[
            pltpu.VMEM((FL * CHUNK, TILE), f32),
            pltpu.SemaphoreType.DMA((N_LON,)),
        ],
        compiler_params=pltpu.CompilerParams(vmem_limit_bytes=VMEM_LARGE),
        name="spread",
    )(lon, grid, stencil, weight, owner, slot)


def table_kernel(order_ref, norm_ref, sine_ref, logcos_ref, high_ref, low_ref, ring):
    order = order_ref[...]
    order_wide = jnp.concatenate([order] * GROUPS, axis=1)
    norm_wide = jnp.concatenate([norm_ref[...]] * GROUPS, axis=1)
    sine = jnp.broadcast_to(sine_ref[...], (8, HALF))
    exponent = norm_wide + order_wide * logcos_ref[...]
    kept = exponent >= -60.0
    diagonal = jnp.where(kept, jnp.exp(jnp.where(kept, exponent, 0.0)), 0.0)
    order_sq = order * order

    def scale_of(degree):
        return jnp.sqrt(
            jnp.maximum(4.0 * degree * degree - 1.0, 1.0)
            / jnp.maximum(degree * degree - order_sq, 1.0)
        )

    def advance(block, carried):
        previous, earlier, scale_prev = carried
        for local in range(32):
            degree = order + (block * 32 + local).astype(f32)
            scale = scale_of(degree)
            ratio = scale / scale_prev
            wide = jnp.concatenate([scale] * GROUPS, axis=1)
            wide_ratio = jnp.concatenate([ratio] * GROUPS, axis=1)
            stepped = (wide * sine) * previous - wide_ratio * earlier
            if local == 0:
                stepped = jnp.where(block == 0, diagonal, stepped)
            slot = (local % 2) * 16 + local // 2
            for v in range(GROUPS):
                at = v * 256 + slot * 8
                ring[at : at + 8, :] = stepped[:, v * TILE : (v + 1) * TILE]
            earlier = previous
            previous = stepped
            scale_prev = scale
        for g in range(GROUPS):

            @pl.when(block * 16 < DEG_USED[g])
            def _():
                for parity in range(2):
                    rows = jnp.concatenate(
                        [
                            ring[pl.ds(v * 256 + parity * 128 + g, 16, stride=8), :]
                            for v in range(GROUPS)
                        ],
                        axis=1,
                    )
                    high, low = split(rows)
                    start = pl.multiple_of(
                        DEG_BASE[g] + parity * DEG_PAD[g] + block * 16, 16
                    )
                    high_ref[pl.ds(start, 16), :] = high
                    low_ref[pl.ds(start, 16), :] = low

        return previous, earlier, scale_prev

    for g in range(GROUPS):
        extra = DEG_PAD[g] - DEG_USED[g]
        if extra:
            for parity in range(2):
                start = DEG_BASE[g] + parity * DEG_PAD[g] + DEG_USED[g]
                high_ref[start : start + extra, :] = jnp.zeros((extra, HALF), bf16)
                low_ref[start : start + extra, :] = jnp.zeros((extra, HALF), bf16)
    blank = jnp.zeros((8, HALF), f32)
    lax.fori_loop(0, NM // 32, advance, (blank, blank, jnp.ones((8, TILE), f32)))


def table_call(order, norm, sine, logcos):
    shape = jax.ShapeDtypeStruct((DEG_TOTAL, HALF), bf16)
    return pl.pallas_call(
        table_kernel,
        out_shape=(shape, shape),
        scratch_shapes=[pltpu.VMEM((GROUPS * 256, TILE), f32)],
        compiler_params=pltpu.CompilerParams(vmem_limit_bytes=VMEM),
        cost_estimate=pl.CostEstimate(
            flops=640 * 5120 * 20, bytes_accessed=6_000_000, transcendentals=640 * 2048
        ),
        name="legendre_table",
    )(order, norm, sine, logcos)


def fourier_kernel(south_ref, extra_ref, *refs):
    chunks = refs[:N_LON]
    stored = refs[N_LON : N_LON + 4]
    bands = refs[N_LON + 4 : N_LON + 7]
    out_hbm = refs[N_LON + 7]
    scratch = refs[N_LON + 8 :]
    sums = scratch[:CHAINS]
    c_high, c_low, tiles, lines, whole, keys, dense_ref, out_ref = scratch[CHAINS : CHAINS + 8]
    tables = scratch[CHAINS + 8 : CHAINS + 12]
    key_sems, tile_sems, table_sems, band_sems, out_sems = scratch[CHAINS + 12 :]
    real_high, real_low, mixed_high, mixed_low = tables
    key_loads = [
        pltpu.make_async_copy(
            chunks[k].at[pl.ds(TILES, 8), :], lines.at[pl.ds(8 * k, 8), :], key_sems.at[k]
        )
        for k in range(N_LON)
    ]
    tile_loads = [
        pltpu.make_async_copy(chunks[k].at[pl.ds(0, TILES), :], tiles.at[k], tile_sems.at[k])
        for k in range(N_LON)
    ]
    table_loads = [
        pltpu.make_async_copy(stored[i], tables[i], table_sems.at[i]) for i in range(4)
    ]
    for copy in key_loads + tile_loads + table_loads:
        copy.start()
    for copy in key_loads:
        copy.wait()
    whole[...] = lines[...].astype(jnp.int32)
    to_scalars = pltpu.make_async_copy(whole, keys, key_sems.at[N_LON])
    to_scalars.start()
    for chain in sums:
        chain[...] = jnp.zeros(chain.shape, f32)
    to_scalars.wait()
    for copy in tile_loads:
        copy.wait()
    share = N_LON // CHAINS
    for part in range(share):
        for line, count in ((0, TILE), (1, TILES - TILE)):

            def scatter(t, _):
                for c, chain in enumerate(sums):
                    k = c * share + part
                    slot = keys[8 * k + line, t]
                    tile = tiles[k, pl.ds(line * TILE + t, 1), :]
                    chain[pl.ds(slot, 1), :] = chain[pl.ds(slot, 1), :] + tile
                return 0

            lax.fori_loop(0, count, scatter, 0, unroll=8)
    south = south_ref[0]
    root = math.sqrt(0.5)
    blank = jnp.zeros((16, NLON), bf16)
    c_high[240:256, :] = blank
    c_low[240:256, :] = blank

    def butterfly(item, _):
        place = item // 5
        chunk = item % 5
        band = jnp.where(south == 1, 2 - place, place)
        row = pl.multiple_of(place * ROWS + chunk * 16, 16)

        def put(column, values):
            high, low = split(values)
            c_high[pl.ds(row, 16), column : column + TILE] = high
            c_low[pl.ds(row, 16), column : column + TILE] = low

        for k in range(TPR):
            d = []
            for b in range(N_LON):
                start = pl.multiple_of(
                    band * DENSE + (b * TPR + k) * ROWS + chunk * 16, 16
                )
                total = sums[0][pl.ds(start, 16), :]
                for chain in sums[1:]:
                    total = total + chain[pl.ds(start, 16), :]
                dense_ref[pl.ds(start, 16), :] = total
                d.append(total)
            s = [d[i] + d[i + 4] for i in range(4)]
            t = [d[i] - d[i + 4] for i in range(4)]
            even, odd = s[0] + s[2], s[1] + s[3]
            minus = (t[1] - t[3]) * root
            plus = (t[1] + t[3]) * root
            at = k * TILE
            put(at, even + odd)
            put(BAND + at, even - odd)
            put(2 * BAND + at, t[0] + minus)
            put(3 * BAND + at, -t[2] - plus)
            put(4 * BAND + at, s[0] - s[2])
            put(5 * BAND + at, s[3] - s[1])
            put(6 * BAND + at, t[0] - minus)
            put(7 * BAND + at, t[2] - plus)
        return 0

    lax.fori_loop(0, 15, butterfly, 0)
    stores = [
        pltpu.make_async_copy(
            dense_ref.at[pl.ds(i * DENSE, DENSE), :], bands[i], band_sems.at[i]
        )
        for i in range(3)
    ]
    for copy in stores:
        copy.start()
    extra = extra_ref[...]
    for copy in table_loads:
        copy.wait()

    def emit(m1, block):
        block = jnp.concatenate([block[:, :TILE], block[:, TILE:] + extra], axis=1)
        for h in range(N_LAT):
            for g in range(GROUPS):
                start = h * WAVE_DEV + 2 * g
                out_ref[m1, h, g, :, :] = block[start : start + 2, :]
        sent = pltpu.make_async_copy(out_ref.at[m1], out_hbm.at[:, m1], out_sems.at[m1])
        sent.start()
        stores.append(sent)

    def transform(ch, cl, wh, wl):
        rows = wh.shape[0]
        both = dot(jnp.concatenate([wh, wl], axis=0), ch, NT)
        return both[:rows] + (both[rows:] + dot(wh, cl, NT))

    for i, m1 in enumerate((0, 4)):
        at = slice(i * BAND, (i + 1) * BAND)
        emit(m1, transform(c_high[:, at], c_low[:, at], real_high[i], real_low[i]))
    for q in (1, 2, 3):
        at = slice(2 * q * BAND, (2 * q + 2) * BAND)
        pair = transform(c_high[:, at], c_low[:, at], mixed_high[q - 1], mixed_low[q - 1])
        emit(q, pair[:160])
        emit(8 - q, pair[160:])
    for copy in stores:
        copy.wait()


def fourier_call(south, chunks, tables, extra):
    vmem = pl.BlockSpec(memory_space=pltpu.VMEM)
    smem = pl.BlockSpec(memory_space=pltpu.SMEM)
    anywhere = pl.BlockSpec(memory_space=pl.ANY)
    result = pl.pallas_call(
        fourier_kernel,
        in_specs=[smem, vmem] + [anywhere] * (N_LON + 4),
        out_specs=[anywhere] * 4,
        out_shape=[jax.ShapeDtypeStruct((DENSE, TILE), f32)] * 3
        + [jax.ShapeDtypeStruct((N_LAT, N_LON, GROUPS, 2, 256), f32)],
        scratch_shapes=[pltpu.VMEM((3 * DENSE, TILE), f32)] * CHAINS
        + [pltpu.VMEM((256, NLON), bf16)] * 2
        + [
            pltpu.VMEM((N_LON, TILES, TILE), f32),
            pltpu.VMEM((8 * N_LON, TILE), f32),
            pltpu.VMEM((8 * N_LON, TILE), jnp.int32),
            pltpu.SMEM((8 * N_LON, TILE), jnp.int32),
            pltpu.VMEM((3 * DENSE, TILE), f32),
            pltpu.VMEM((N_LON, N_LAT, GROUPS, 2, 256), f32),
        ]
        + [pltpu.VMEM(table.shape, table.dtype) for table in tables]
        + [
            pltpu.SemaphoreType.DMA((N_LON + 1,)),
            pltpu.SemaphoreType.DMA((N_LON,)),
            pltpu.SemaphoreType.DMA((4,)),
            pltpu.SemaphoreType.DMA((3,)),
            pltpu.SemaphoreType.DMA((N_LON,)),
        ],
        compiler_params=pltpu.CompilerParams(vmem_limit_bytes=VMEM_LARGE),
        name="scatter_fourier",
    )(south, extra, *chunks, *tables)
    return list(result[:3]) + [result[3].reshape(N_LAT * N_LON, GROUPS, 2, 256)]


def legendre_kernel(
    wave_ref, coeff_ref, high_ref, low_ref, weight_ref, rate_ref, out_ref, north, south, blend
):
    weight = weight_ref[...]
    row16 = lax.broadcasted_iota(jnp.int32, (16, HALF), 0)
    first_level = (row16 // 2) % 2 == 0
    is_first = row16 % 2 == 0
    lane128 = lax.broadcasted_iota(jnp.int32, (16, TILE), 1)
    is_blend = lane128 >= TILE - 16

    def mixed(values, own, cross):
        ahead = pltpu.roll(values, 14, 0)
        behind = pltpu.roll(values, 2, 0)
        other = jnp.where(first_level, ahead, behind)
        return values + own * values + cross * other

    pad = jnp.zeros((16, TILE), f32)
    north[...] = jnp.zeros(north.shape, f32)
    south[...] = jnp.zeros(south.shape, f32)
    blend[...] = jnp.zeros(blend.shape, f32)
    for g in range(GROUPS):
        for a in range(N_LAT):
            total, place = (north, a) if a < 8 else (south, 15 - a)
            piece = jnp.concatenate([coeff_ref[a * 8 + f, g, :, :] for f in range(FL)], axis=0)
            last = piece[:, TILE:]
            piece = jnp.concatenate([piece[:, :TILE], jnp.where(is_blend, 0.0, last), pad], axis=1)
            offset = ROWS * place + 48
            base = offset // TILE * TILE
            total[g, :, base : base + 384] += pltpu.roll(piece, offset % TILE, 1)
            offset = ROWS * place + 16 * g
            base = offset // TILE * TILE
            last = pltpu.roll(jnp.where(is_blend, last, 0.0), (offset % TILE + 16) % TILE, 1)
            blend[a // 8, :, base : base + TILE] += last
    blends = []
    for side in range(2):
        both = blend[side]
        blends.append(jnp.where(is_first, both, pltpu.roll(both, 1, 0)))
        blends.append(jnp.where(is_first, pltpu.roll(both, 15, 0), both))
    dn, xn, ds, xs = blends
    for g in range(GROUPS):
        extra_n = north[g, :, 768:896]
        extra_s = south[g, :, 768:896]
        north[g, :, 640:768] += pltpu.roll(extra_s, 48, 1)
        south[g, :, 640:768] += pltpu.roll(extra_n, 48, 1)
        full_n = mixed(north[g, :, 128:768], dn, xn)
        full_s = mixed(south[g, :, 128:768], ds, xs)
        pad_len = DEG_PAD[g]
        wave = wave_ref[0] + 128 * g
        factor = jnp.where(wave == 0, 1.0, 2.0).astype(f32)
        lane = lax.broadcasted_iota(jnp.int32, (16, pad_len), 1)
        rate = jnp.concatenate([rate_ref[...]] * (pad_len // TILE), axis=1)
        results = []
        for parity, folded in enumerate((full_n + full_s, full_n - full_s)):
            skip = LANES[g]
            both = stacked_parts((folded * weight)[:, skip:])
            start = DEG_BASE[g] + parity * pad_len
            ph = high_ref[start : start + pad_len, skip:]
            pw = low_ref[start : start + pad_len, skip:]
            main = dot(both, ph, NT)
            spectrum = main[:16] + (main[16:] + dot(both[:16], pw, NT))
            degree = wave + parity + 2 * lane
            degree_f = degree.astype(f32)
            ratio = rate * (degree_f * (degree_f + 1.0) / float(NM * (NM + 1)))
            damped = spectrum * (-ratio / (1.0 + ratio)) * factor
            damped = jnp.where(degree < NM, damped, 0.0)
            both = stacked_parts(damped)
            main = dot(both, ph, NN)
            grid = main[:16] + (main[16:] + dot(both[:16], pw, NN))
            if skip:
                grid = jnp.concatenate([jnp.zeros((16, skip), f32), grid], axis=1)
            results.append(grid)
        for a in range(N_LAT):
            place = a if a < 8 else 15 - a
            offset = ROWS * place
            base = offset // TILE * TILE
            shift = offset % TILE
            width = TILE if shift <= 48 else 256
            even = results[0][:, base : base + width]
            odd = results[1][:, base : base + width]
            piece = even + odd if a < 8 else even - odd
            if shift:
                piece = pltpu.roll(piece, width - shift, 1)
            for f in range(FL):
                out_ref[a * 8 + f, g, :, :] = piece[2 * f : 2 * f + 2, :TILE]


def legendre_call(wave, coeff, high, low, weight, rate):
    vmem = pl.BlockSpec(memory_space=pltpu.VMEM)
    smem = pl.BlockSpec(memory_space=pltpu.SMEM)
    return pl.pallas_call(
        legendre_kernel,
        in_specs=[smem] + [vmem] * 5,
        out_specs=vmem,
        out_shape=jax.ShapeDtypeStruct((N_LAT * N_LON, GROUPS, 2, TILE), f32),
        scratch_shapes=[pltpu.VMEM((GROUPS, 16, 896), f32)] * 2
        + [pltpu.VMEM((2, 16, HALF), f32)],
        compiler_params=pltpu.CompilerParams(vmem_limit_bytes=VMEM),
        name="legendre",
    )(wave, coeff, high, low, weight, rate)


def synthesis_kernel(back_ref, real_high, real_low, mixed_high, mixed_low, synth, waves):
    for m1 in range(8):
        for h in range(N_LAT):
            for g in range(GROUPS):
                start = m1 * 160 + h * WAVE_DEV + 2 * g
                waves[start : start + 2, :] = back_ref[h * 8 + m1, g, :, :]

    def transform(parts, wh, wl):
        stacked = jnp.concatenate([waves[m1 * 160 : m1 * 160 + 160, :] for m1 in parts], axis=0)
        both = stacked_parts(stacked.T[:ROWS, :])
        main = dot(both, wh, NN)
        return main[:ROWS] + (main[ROWS:] + dot(both[:ROWS], wl, NN))

    for i, m1 in enumerate((0, 4)):
        synth[:, i * BAND : (i + 1) * BAND] = transform((m1,), real_high[i], real_low[i])
    for q in (1, 2, 3):
        synth[:, 2 * q * BAND : (2 * q + 2) * BAND] = transform(
            (q, 8 - q), mixed_high[q - 1], mixed_low[q - 1]
        )


def synthesis_call(back, tables):
    vmem = pl.BlockSpec(memory_space=pltpu.VMEM)
    return pl.pallas_call(
        synthesis_kernel,
        in_specs=[vmem] * 5,
        out_specs=vmem,
        out_shape=jax.ShapeDtypeStruct((ROWS, NLON), f32),
        scratch_shapes=[pltpu.VMEM((8 * 160, TILE), f32)],
        compiler_params=pltpu.CompilerParams(vmem_limit_bytes=VMEM),
        cost_estimate=pl.CostEstimate(
            flops=6 * 80 * 860_160, bytes_accessed=8_000_000, transcendentals=0
        ),
        name="wave_synthesis",
    )(back, *tables)


def combine_kernel(lon_ref, synth, own_ref, other_ref, mix_ref, *rest):
    outs, (out_ref, sems) = rest[:N_LON], rest[N_LON:]
    root = math.sqrt(0.5)

    def combine(chunk, _):
        row = pl.multiple_of(chunk * 16, 16)
        diag = mix_ref[0, pl.ds(row, 16), :]
        cross = mix_ref[1, pl.ds(row, 16), :]
        for k in range(TPR):
            y = [
                synth[pl.ds(row, 16), i * BAND + k * TILE : i * BAND + (k + 1) * TILE]
                for i in range(8)
            ]
            e0, e1 = y[0] + y[1], y[0] - y[1]
            r1, i1, r2, i2, r3, i3 = y[2:]
            even = (e0 + r2, e1 - i2, e0 - r2, e1 + i2)
            odd = (
                r1 + r3,
                ((r1 - i1) - (r3 + i3)) * root,
                i3 - i1,
                ((r3 - i3) - (r1 + i1)) * root,
            )
            for b in range(N_LON):
                at = pl.multiple_of((b * TPR + k) * ROWS + chunk * 16, 16)
                own = own_ref[pl.ds(at, 16), :]
                diffused = own + diag * own + cross * other_ref[pl.ds(at, 16), :]
                wave = even[b % 4] + odd[b % 4] if b < 4 else even[b % 4] - odd[b % 4]
                out_ref[pl.ds(at, 16), :] = diffused + wave
        return 0

    lax.fori_loop(0, ROWS // 16, combine, 0)
    exchange = [
        pltpu.make_async_copy(
            out_ref.at[pl.ds(pl.multiple_of((lon_ref[0] ^ k) * TILES, 8), TILES), :],
            outs[k],
            sems.at[k],
        )
        for k in range(N_LON)
    ]
    for copy in exchange:
        copy.start()
    for copy in exchange:
        copy.wait()


def combine_call(lon, synth, own, other, mix):
    vmem = pl.BlockSpec(memory_space=pltpu.VMEM)
    smem = pl.BlockSpec(memory_space=pltpu.SMEM)
    return pl.pallas_call(
        combine_kernel,
        in_specs=[smem] + [vmem] * 4,
        out_specs=[pl.BlockSpec(memory_space=pl.ANY)] * N_LON,
        out_shape=[jax.ShapeDtypeStruct((TILES, TILE), f32)] * N_LON,
        scratch_shapes=[
            pltpu.VMEM((DENSE, TILE), f32),
            pltpu.SemaphoreType.DMA((N_LON,)),
        ],
        compiler_params=pltpu.CompilerParams(vmem_limit_bytes=VMEM),
        name="combine",
    )(lon, synth, own, other, mix)


def place_kernel(south_ref, lon_ref, *rest):
    chunks, (out_ref, rows_ref, sems) = rest[:N_LON], rest[N_LON:]
    south = south_ref[0]
    loads = [
        pltpu.make_async_copy(
            chunks[k],
            rows_ref.at[pl.ds(pl.multiple_of((lon_ref[0] ^ k) * TILES, 8), TILES), :],
            sems.at[k],
        )
        for k in range(N_LON)
    ]
    for copy in loads:
        copy.start()
    for copy in loads:
        copy.wait()

    def place(i, _):
        target = jnp.where(south == 1, ROWS - 1 - i, i)
        for k in range(TPR):
            out_ref[target, :, k * TILE : (k + 1) * TILE] = rows_ref[
                pl.ds(k * ROWS + i, FL, stride=TILES), :
            ]
        return 0

    lax.fori_loop(0, ROWS, place, 0, unroll=8)


def place_call(south, lon, chunks):
    vmem = pl.BlockSpec(memory_space=pltpu.VMEM)
    smem = pl.BlockSpec(memory_space=pltpu.SMEM)
    return pl.pallas_call(
        place_kernel,
        in_specs=[smem, smem] + [pl.BlockSpec(memory_space=pl.ANY)] * N_LON,
        out_specs=vmem,
        out_shape=jax.ShapeDtypeStruct((ROWS, FL, BAND), f32),
        scratch_shapes=[
            pltpu.VMEM((FL * TILES, TILE), f32),
            pltpu.SemaphoreType.DMA((N_LON,)),
        ],
        compiler_params=pltpu.CompilerParams(vmem_limit_bytes=VMEM),
        name="place_rows",
    )(south, lon, *chunks)


def local(
    adjoint_grid, tile_owner, tile_slot, stencil, interp_weight, vertical_offset, diffusion_rate
):
    lat_here = lax.axis_index("lat")
    lon_here = lax.axis_index("lon")
    is_south = lat_here >= N_LAT // 2
    south = is_south.astype(jnp.int32).reshape(1)
    wave = (lon_here + 8 * lat_here).astype(jnp.int32)

    mix = vertical_offset.reshape(ROWS, 16)
    mix = jnp.where(is_south, jnp.flip(mix, 0), mix).T
    level = lon_here % 2
    field = lon_here // 2
    own_row = lax.dynamic_index_in_dim(mix, field * 4 + level * 3, 0, False)
    cross_row = lax.dynamic_index_in_dim(mix, field * 4 + (1 - level) * 2 + level, 0, False)
    blend = jnp.stack([own_row, cross_row])
    mix_grid = jnp.broadcast_to(blend[:, :, None], (2, ROWS, TILE))
    extra = blend.reshape(2, GROUPS, 16).transpose(1, 0, 2).reshape(WAVE_DEV, 16)
    extra = jnp.pad(jnp.tile(extra, (N_LAT, 1)), ((0, 0), (TILE - 16, 0)))

    latitude = 0.5 * math.pi - math.pi * (np.arange(HALF) + 0.5) / NLAT
    sine = jnp.asarray(np.sin(latitude)[None, :], f32)
    logcos = jnp.asarray(np.log(np.cos(latitude))[None, :], f32)
    weight = jnp.asarray((math.pi / NLAT * np.cos(latitude) / NLON)[None, :], f32)
    groups = np.zeros((TILE, 8))
    groups[:, :GROUPS] = log_norms().reshape(GROUPS, TILE).T
    norm = lax.dynamic_index_in_dim(jnp.asarray(groups, f32), wave, 0, False)
    norm = jnp.broadcast_to(norm[:, None], (8, TILE))
    group_start = jnp.minimum(jnp.arange(8, dtype=jnp.int32), GROUPS - 1) * TILE
    order = jnp.broadcast_to((wave + group_start).astype(f32)[:, None], (8, TILE))
    rate = jnp.broadcast_to(
        jnp.repeat(diffusion_rate, 2, total_repeat_length=16)[:, None], (16, TILE)
    )
    real, mixed = wave_tables()
    tables = tuple(jnp.asarray(part) for part in two_parts(real) + two_parts(mixed))

    lon = lon_here.astype(jnp.int32).reshape(1)

    def exchanged(chunks):
        return [chunks[0]] + [
            lax.ppermute(chunks[k], "lon", [(i, i ^ k) for i in range(N_LON)])
            for k in range(1, N_LON)
        ]

    chunks = exchanged(spread_call(
        jnp.stack([lon_here, lat_here]).astype(jnp.int32),
        adjoint_grid,
        stencil,
        interp_weight,
        tile_owner.reshape(1, TILES),
        tile_slot.reshape(1, TILES),
    ))
    high, low = table_call(order, norm, sine, logcos)
    tables, high, low, extra, rate, mix_grid = lax.optimization_barrier(
        (tables, high, low, extra, rate, mix_grid)
    )
    dense_below, dense_here, dense_above, coeff = fourier_call(south, chunks, tables, extra)
    coeff = lax.all_to_all(coeff, ("lat", "lon"), 0, 0, tiled=True)
    dense_below, dense_above, coeff = lax.optimization_barrier((dense_below, dense_above, coeff))
    below = lax.ppermute(dense_below, "lat", [(i + 1, i) for i in range(N_LAT - 1)])
    above = lax.ppermute(dense_above, "lat", [(i, i + 1) for i in range(N_LAT - 1)])
    back = legendre_call(wave.reshape(1), coeff, high, low, weight, rate)
    back = lax.all_to_all(back, ("lat", "lon"), 0, 0, tiled=True)
    dense_here, back = lax.optimization_barrier((dense_here, back))
    departed = dense_here + below + above
    other = lax.ppermute(departed, "lon", [(i, i ^ 1) for i in range(N_LON)])
    synth = synthesis_call(back, tables)
    result = exchanged(combine_call(lon, synth, departed, other, mix_grid))
    return place_call(south, lon, result)


def solution(mesh):
    in_specs = (
        P("lat", None, "lon"),
        P("lat", "lon", None, None),
        P("lat", "lon", None, None),
        P("lat", "lon", None, None),
        P("lat", "lon", None, None),
        P("lat", None, None, None),
        P(),
    )
    out_specs = P("lat", None, "lon")
    return jax.shard_map(local, mesh=mesh, in_specs=in_specs, out_specs=out_specs, check_vma=False)
```

```python
import math

import jax
import jax.numpy as jnp
import ml_dtypes
import numpy as np
from jax import lax
from jax.experimental import pallas as pl
from jax.experimental.pallas import tpu as pltpu
from jax.sharding import PartitionSpec as P

NLAT = 1280
NLON = 3072
NM = 640
FL = 8
STEN = 4
TILE = 128
ROWS = 80
TPR = 3
TILES = 240
N_LAT = 16
N_LON = 8
HALF = NLAT // 2
BAND = NLON // N_LON
GROUPS = 5
WAVE_DEV = 2 * GROUPS
DENSE = N_LON * TPR * ROWS
CHUNK = TILES + 8
CHAINS = 4
DEG_PAD = (384, 256, 256, 128, 128)
DEG_USED = (320, 256, 192, 128, 64)
DEG_BASE = (0, 768, 1280, 1792, 2048)
DEG_TOTAL = 2304
VMEM = 40 * 1024 * 1024
VMEM_LARGE = 60 * 1024 * 1024

f32 = jnp.float32
bf16 = jnp.bfloat16
NT = (((1,), (1,)), ((), ()))
NN = (((1,), (0,)), ((), ()))


def two_parts(values):
    high = values.astype(ml_dtypes.bfloat16)
    low = (values - high.astype(np.float64)).astype(ml_dtypes.bfloat16)
    return high, low


def wave_tables():
    h = np.arange(N_LAT)[:, None]
    g = np.arange(GROUPS)[None, :]
    points = np.arange(BAND)

    def angle(m1):
        waves = (m1 + 8 * h + 128 * g).reshape(-1)
        return (waves[:, None] * points[None, :] % NLON) * (2.0 * math.pi / NLON)

    def rows(first, second):
        return np.stack([first, second], axis=1).reshape(-1, first.shape[-1])

    real = np.stack([rows(np.cos(angle(m1)), -np.sin(angle(m1))) for m1 in (0, 4)])
    mixed = []
    for q in (1, 2, 3):
        a, b = angle(q), angle(8 - q)
        upper = rows(
            np.concatenate([np.cos(a), np.sin(a)], 1), np.concatenate([-np.sin(a), np.cos(a)], 1)
        )
        lower = rows(
            np.concatenate([np.cos(b), -np.sin(b)], 1),
            np.concatenate([-np.sin(b), -np.cos(b)], 1),
        )
        mixed.append(np.concatenate([upper, lower], 0))
    return real, np.stack(mixed)


def log_norms():
    return np.array(
        [
            0.5 * (math.lgamma(m + 1.5) - math.lgamma(m + 1.0) - 0.5 * math.log(math.pi))
            for m in range(NM)
        ]
    )


def first_lanes():
    latitude = 0.5 * math.pi - math.pi * (np.arange(HALF) + 0.5) / NLAT
    exponent = log_norms()[:, None] + np.arange(NM)[:, None] * np.log(np.cos(latitude))[None, :]
    firsts = np.argmax(exponent >= -61.0, axis=1).reshape(GROUPS, NM // GROUPS).min(axis=1)
    return [int(first) // TILE * TILE for first in firsts]


LANES = first_lanes()


def split(values):
    high = values.astype(bf16)
    low = (values - high.astype(f32)).astype(bf16)
    return high, low


def stacked_parts(values):
    high = values.astype(bf16).astype(f32)
    return jnp.concatenate([high, values - high], axis=0).astype(bf16)


def dot(a, b, dims):
    return lax.dot_general(a, b, dims, preferred_element_type=f32)


def spread_kernel(lon_ref, grid_ref, stencil_ref, weight_ref, owner_ref, slot_ref, *rest):
    outs, (out_ref, sems) = rest[:N_LON], rest[N_LON:]
    block = grid_ref.shape[0]
    step = pl.program_id(0)
    target = lax.broadcasted_iota(jnp.int32, (TILE, TILE), 0).astype(jnp.int16)

    def tall(row, kind):
        block16 = jnp.broadcast_to(row, (16, TILE)).astype(kind)
        return jnp.concatenate([block16] * (TILE // 16), axis=0)

    for r in range(block):
        for k in range(TPR):
            field = grid_ref[r, :, k * TILE : (k + 1) * TILE]
            points = [stencil_ref[r, k, s : s + 1, :] for s in range(STEN)]
            weights = [weight_ref[r, k, s : s + 1, :] for s in range(STEN)]
            for s in range(STEN):
                for later in range(s + 1, STEN):
                    weights[s] = weights[s] + jnp.where(
                        points[later] == points[s], weight_ref[r, k, later : later + 1, :], 0.0
                    )
            high = jnp.zeros((TILE, TILE), bf16)
            low = high
            for s in reversed(range(STEN)):
                top = weights[s].astype(bf16).astype(f32)
                here = tall(points[s], jnp.int16) == target
                high = jnp.where(here, tall(top, bf16), high)
                low = jnp.where(here, tall(weights[s] - top, bf16), low)
            top = field.astype(bf16).astype(f32)
            sides = jnp.concatenate(
                [
                    jnp.concatenate([top, field - top], axis=0),
                    jnp.concatenate([top, jnp.zeros_like(top)], axis=0),
                ],
                axis=1,
            ).astype(bf16)
            both = dot(sides, jnp.concatenate([high, low], axis=1), NT)
            tile = step * (block * TPR) + r * TPR + k
            out_ref[pl.ds(tile, FL, stride=CHUNK), :] = both[:FL] + both[FL:]

    @pl.when(step == pl.num_programs(0) - 1)
    def _():
        owner, slot = owner_ref[...], slot_ref[...]
        dest_lat = owner // N_LON
        line = (slot * 171) // 512
        column = (owner - dest_lat * N_LON) * TPR + slot - line * TPR
        line = jnp.where(dest_lat >= N_LAT // 2, ROWS - 1 - line, line)
        keys = ((dest_lat - lon_ref[1] + 1) * (N_LON * TPR) + column) * ROWS + line
        keys = keys.astype(f32)
        for f in range(FL):
            at = f * CHUNK + TILES
            out_ref[at : at + 8, :] = jnp.zeros((8, TILE), f32)
            out_ref[at : at + 1, :] = keys[:, :TILE]
            out_ref[at + 1 : at + 2, : TILES - TILE] = keys[:, TILE:]
        exchange = [
            pltpu.make_async_copy(
                out_ref.at[pl.ds(pl.multiple_of((lon_ref[0] ^ k) * CHUNK, 8), CHUNK), :],
                outs[k],
                sems.at[k],
            )
            for k in range(N_LON)
        ]
        for copy in exchange:
            copy.start()
        for copy in exchange:
            copy.wait()


def spread_call(lon, grid, stencil, weight, owner, slot):
    block = 40
    return pl.pallas_call(
        spread_kernel,
        grid=(ROWS // block,),
        in_specs=[
            pl.BlockSpec(memory_space=pltpu.SMEM),
            pl.BlockSpec((block, FL, BAND), lambda i: (i, 0, 0)),
            pl.BlockSpec((block, TPR, STEN, TILE), lambda i: (i, 0, 0, 0)),
            pl.BlockSpec((block, TPR, STEN, TILE), lambda i: (i, 0, 0, 0)),
            pl.BlockSpec((1, TILES), lambda i: (0, 0)),
            pl.BlockSpec((1, TILES), lambda i: (0, 0)),
        ],
        out_specs=[pl.BlockSpec(memory_space=pl.ANY)] * N_LON,
        out_shape=[jax.ShapeDtypeStruct((CHUNK, TILE), f32)] * N_LON,
        scratch_shapes=[
            pltpu.VMEM((FL * CHUNK, TILE), f32),
            pltpu.SemaphoreType.DMA((N_LON,)),
        ],
        compiler_params=pltpu.CompilerParams(vmem_limit_bytes=VMEM_LARGE),
        name="spread",
    )(lon, grid, stencil, weight, owner, slot)


def table_kernel(order_ref, norm_ref, sine_ref, logcos_ref, high_ref, low_ref, ring):
    order = order_ref[...]
    order_wide = jnp.concatenate([order] * GROUPS, axis=1)
    norm_wide = jnp.concatenate([norm_ref[...]] * GROUPS, axis=1)
    sine = jnp.broadcast_to(sine_ref[...], (8, HALF))
    exponent = norm_wide + order_wide * logcos_ref[...]
    kept = exponent >= -60.0
    diagonal = jnp.where(kept, jnp.exp(jnp.where(kept, exponent, 0.0)), 0.0)
    order_sq = order * order

    def scale_of(degree):
        return jnp.sqrt(
            jnp.maximum(4.0 * degree * degree - 1.0, 1.0)
            / jnp.maximum(degree * degree - order_sq, 1.0)
        )

    def advance(block, carried):
        previous, earlier, scale_prev = carried
        for local in range(32):
            degree = order + (block * 32 + local).astype(f32)
            scale = scale_of(degree)
            ratio = scale / scale_prev
            wide = jnp.concatenate([scale] * GROUPS, axis=1)
            wide_ratio = jnp.concatenate([ratio] * GROUPS, axis=1)
            stepped = (wide * sine) * previous - wide_ratio * earlier
            if local == 0:
                stepped = jnp.where(block == 0, diagonal, stepped)
            slot = (local % 2) * 16 + local // 2
            for v in range(GROUPS):
                at = v * 256 + slot * 8
                ring[at : at + 8, :] = stepped[:, v * TILE : (v + 1) * TILE]
            earlier = previous
            previous = stepped
            scale_prev = scale
        for g in range(GROUPS):

            @pl.when(block * 16 < DEG_USED[g])
            def _():
                for parity in range(2):
                    rows = jnp.concatenate(
                        [
                            ring[pl.ds(v * 256 + parity * 128 + g, 16, stride=8), :]
                            for v in range(GROUPS)
                        ],
                        axis=1,
                    )
                    high, low = split(rows)
                    start = pl.multiple_of(
                        DEG_BASE[g] + parity * DEG_PAD[g] + block * 16, 16
                    )
                    high_ref[pl.ds(start, 16), :] = high
                    low_ref[pl.ds(start, 16), :] = low

        return previous, earlier, scale_prev

    for g in range(GROUPS):
        extra = DEG_PAD[g] - DEG_USED[g]
        if extra:
            for parity in range(2):
                start = DEG_BASE[g] + parity * DEG_PAD[g] + DEG_USED[g]
                high_ref[start : start + extra, :] = jnp.zeros((extra, HALF), bf16)
                low_ref[start : start + extra, :] = jnp.zeros((extra, HALF), bf16)
    blank = jnp.zeros((8, HALF), f32)
    lax.fori_loop(0, NM // 32, advance, (blank, blank, jnp.ones((8, TILE), f32)))


def table_call(order, norm, sine, logcos):
    shape = jax.ShapeDtypeStruct((DEG_TOTAL, HALF), bf16)
    return pl.pallas_call(
        table_kernel,
        out_shape=(shape, shape),
        scratch_shapes=[pltpu.VMEM((GROUPS * 256, TILE), f32)],
        compiler_params=pltpu.CompilerParams(vmem_limit_bytes=VMEM),
        cost_estimate=pl.CostEstimate(
            flops=640 * 5120 * 20, bytes_accessed=6_000_000, transcendentals=640 * 2048
        ),
        name="legendre_table",
    )(order, norm, sine, logcos)


def fourier_kernel(south_ref, extra_ref, *refs):
    chunks = refs[:N_LON]
    stored = refs[N_LON : N_LON + 4]
    bands = refs[N_LON + 4 : N_LON + 7]
    out_hbm = refs[N_LON + 7]
    scratch = refs[N_LON + 8 :]
    sums = scratch[:CHAINS]
    c_high, c_low, tiles, lines, whole, keys, dense_ref, out_ref = scratch[CHAINS : CHAINS + 8]
    tables = scratch[CHAINS + 8 : CHAINS + 12]
    key_sems, tile_sems, table_sems, band_sems, out_sems = scratch[CHAINS + 12 :]
    real_high, real_low, mixed_high, mixed_low = tables
    key_loads = [
        pltpu.make_async_copy(
            chunks[k].at[pl.ds(TILES, 8), :], lines.at[pl.ds(8 * k, 8), :], key_sems.at[k]
        )
        for k in range(N_LON)
    ]
    tile_loads = [
        pltpu.make_async_copy(chunks[k].at[pl.ds(0, TILES), :], tiles.at[k], tile_sems.at[k])
        for k in range(N_LON)
    ]
    table_loads = [
        pltpu.make_async_copy(stored[i], tables[i], table_sems.at[i]) for i in range(4)
    ]
    for copy in key_loads + tile_loads + table_loads:
        copy.start()
    for copy in key_loads:
        copy.wait()
    whole[...] = lines[...].astype(jnp.int32)
    to_scalars = pltpu.make_async_copy(whole, keys, key_sems.at[N_LON])
    to_scalars.start()
    for chain in sums:
        chain[...] = jnp.zeros(chain.shape, f32)
    to_scalars.wait()
    for copy in tile_loads:
        copy.wait()
    share = N_LON // CHAINS
    for part in range(share):
        for line, count in ((0, TILE), (1, TILES - TILE)):

            def scatter(t, _):
                for c, chain in enumerate(sums):
                    k = c * share + part
                    slot = keys[8 * k + line, t]
                    tile = tiles[k, pl.ds(line * TILE + t, 1), :]
                    chain[pl.ds(slot, 1), :] = chain[pl.ds(slot, 1), :] + tile
                return 0

            lax.fori_loop(0, count, scatter, 0, unroll=16)
    south = south_ref[0]
    root = math.sqrt(0.5)
    blank = jnp.zeros((16, NLON), bf16)
    c_high[240:256, :] = blank
    c_low[240:256, :] = blank

    def butterfly(band, chunk):
        place = jnp.where(south == 1, 2 - band, band)
        row = pl.multiple_of(place * ROWS + chunk * 16, 16)

        def put(column, values):
            high, low = split(values)
            c_high[pl.ds(row, 16), column : column + TILE] = high
            c_low[pl.ds(row, 16), column : column + TILE] = low

        for k in range(TPR):
            d = []
            for b in range(N_LON):
                start = pl.multiple_of(
                    band * DENSE + (b * TPR + k) * ROWS + chunk * 16, 16
                )
                total = sums[0][pl.ds(start, 16), :]
                for chain in sums[1:]:
                    total = total + chain[pl.ds(start, 16), :]
                dense_ref[pl.ds(start, 16), :] = total
                d.append(total)
            s = [d[i] + d[i + 4] for i in range(4)]
            t = [d[i] - d[i + 4] for i in range(4)]
            even, odd = s[0] + s[2], s[1] + s[3]
            minus = (t[1] - t[3]) * root
            plus = (t[1] + t[3]) * root
            at = k * TILE
            put(at, even + odd)
            put(BAND + at, even - odd)
            put(2 * BAND + at, t[0] + minus)
            put(3 * BAND + at, -t[2] - plus)
            put(4 * BAND + at, s[0] - s[2])
            put(5 * BAND + at, s[3] - s[1])
            put(6 * BAND + at, t[0] - minus)
            put(7 * BAND + at, t[2] - plus)

    stores = []
    for band in range(3):

        def step(chunk, _, band=band):
            butterfly(band, chunk)
            return 0

        lax.fori_loop(0, ROWS // 16, step, 0)
        sent = pltpu.make_async_copy(
            dense_ref.at[pl.ds(band * DENSE, DENSE), :], bands[band], band_sems.at[band]
        )
        sent.start()
        stores.append(sent)
    extra = extra_ref[...]
    for copy in table_loads:
        copy.wait()

    def emit(m1, block):
        block = jnp.concatenate([block[:, :TILE], block[:, TILE:] + extra], axis=1)
        for h in range(N_LAT):
            for g in range(GROUPS):
                start = h * WAVE_DEV + 2 * g
                out_ref[m1, h, g, :, :] = block[start : start + 2, :]
        sent = pltpu.make_async_copy(out_ref.at[m1], out_hbm.at[:, m1], out_sems.at[m1])
        sent.start()
        stores.append(sent)

    def transform(ch, cl, wh, wl):
        rows = wh.shape[0]
        both = dot(jnp.concatenate([wh, wl], axis=0), ch, NT)
        return both[:rows] + (both[rows:] + dot(wh, cl, NT))

    for i, m1 in enumerate((0, 4)):
        at = slice(i * BAND, (i + 1) * BAND)
        emit(m1, transform(c_high[:, at], c_low[:, at], real_high[i], real_low[i]))
    for q in (1, 2, 3):
        at = slice(2 * q * BAND, (2 * q + 2) * BAND)
        pair = transform(c_high[:, at], c_low[:, at], mixed_high[q - 1], mixed_low[q - 1])
        emit(q, pair[:160])
        emit(8 - q, pair[160:])
    for copy in stores:
        copy.wait()


def fourier_call(south, chunks, tables, extra):
    vmem = pl.BlockSpec(memory_space=pltpu.VMEM)
    smem = pl.BlockSpec(memory_space=pltpu.SMEM)
    anywhere = pl.BlockSpec(memory_space=pltpu.HBM)
    result = pl.pallas_call(
        fourier_kernel,
        in_specs=[smem, vmem] + [anywhere] * (N_LON + 4),
        out_specs=[anywhere] * 4,
        out_shape=[jax.ShapeDtypeStruct((DENSE, TILE), f32)] * 3
        + [jax.ShapeDtypeStruct((N_LAT, N_LON, GROUPS, 2, 256), f32)],
        scratch_shapes=[pltpu.VMEM((3 * DENSE, TILE), f32)] * CHAINS
        + [pltpu.VMEM((256, NLON), bf16)] * 2
        + [
            pltpu.VMEM((N_LON, TILES, TILE), f32),
            pltpu.VMEM((8 * N_LON, TILE), f32),
            pltpu.VMEM((8 * N_LON, TILE), jnp.int32),
            pltpu.SMEM((8 * N_LON, TILE), jnp.int32),
            pltpu.VMEM((3 * DENSE, TILE), f32),
            pltpu.VMEM((N_LON, N_LAT, GROUPS, 2, 256), f32),
        ]
        + [pltpu.VMEM(table.shape, table.dtype) for table in tables]
        + [
            pltpu.SemaphoreType.DMA((N_LON + 1,)),
            pltpu.SemaphoreType.DMA((N_LON,)),
            pltpu.SemaphoreType.DMA((4,)),
            pltpu.SemaphoreType.DMA((3,)),
            pltpu.SemaphoreType.DMA((N_LON,)),
        ],
        compiler_params=pltpu.CompilerParams(vmem_limit_bytes=50 * 1024 * 1024),
        name="scatter_fourier",
    )(south, extra, *chunks, *tables)
    return list(result[:3]) + [result[3].reshape(N_LAT * N_LON, GROUPS, 2, 256)]


def legendre_kernel(
    wave_ref, coeff_ref, high_ref, low_ref, weight_ref, rate_ref, out_ref, north, south, blend
):
    weight = weight_ref[...]
    row16 = lax.broadcasted_iota(jnp.int32, (16, HALF), 0)
    first_level = (row16 // 2) % 2 == 0
    is_first = row16 % 2 == 0
    lane128 = lax.broadcasted_iota(jnp.int32, (16, TILE), 1)
    is_blend = lane128 >= TILE - 16

    def mixed(values, own, cross):
        ahead = pltpu.roll(values, 14, 0)
        behind = pltpu.roll(values, 2, 0)
        other = jnp.where(first_level, ahead, behind)
        return values + own * values + cross * other

    pad = jnp.zeros((16, TILE), f32)
    north[...] = jnp.zeros(north.shape, f32)
    south[...] = jnp.zeros(south.shape, f32)
    blend[...] = jnp.zeros(blend.shape, f32)
    for g in range(GROUPS):
        for a in range(N_LAT):
            total, place = (north, a) if a < 8 else (south, 15 - a)
            piece = jnp.concatenate([coeff_ref[a * 8 + f, g, :, :] for f in range(FL)], axis=0)
            last = piece[:, TILE:]
            piece = jnp.concatenate([piece[:, :TILE], jnp.where(is_blend, 0.0, last), pad], axis=1)
            offset = ROWS * place + 48
            base = offset // TILE * TILE
            total[g, :, base : base + 384] += pltpu.roll(piece, offset % TILE, 1)
            offset = ROWS * place + 16 * g
            base = offset // TILE * TILE
            last = pltpu.roll(jnp.where(is_blend, last, 0.0), (offset % TILE + 16) % TILE, 1)
            blend[a // 8, :, base : base + TILE] += last
    blends = []
    for side in range(2):
        both = blend[side]
        blends.append(jnp.where(is_first, both, pltpu.roll(both, 1, 0)))
        blends.append(jnp.where(is_first, pltpu.roll(both, 15, 0), both))
    dn, xn, ds, xs = blends
    for g in range(GROUPS):
        extra_n = north[g, :, 768:896]
        extra_s = south[g, :, 768:896]
        north[g, :, 640:768] += pltpu.roll(extra_s, 48, 1)
        south[g, :, 640:768] += pltpu.roll(extra_n, 48, 1)
        full_n = mixed(north[g, :, 128:768], dn, xn)
        full_s = mixed(south[g, :, 128:768], ds, xs)
        pad_len = DEG_PAD[g]
        wave = wave_ref[0] + 128 * g
        factor = jnp.where(wave == 0, 1.0, 2.0).astype(f32)
        lane = lax.broadcasted_iota(jnp.int32, (16, pad_len), 1)
        rate = jnp.concatenate([rate_ref[...]] * (pad_len // TILE), axis=1)
        results = []
        for parity, folded in enumerate((full_n + full_s, full_n - full_s)):
            skip = LANES[g]
            both = stacked_parts((folded * weight)[:, skip:])
            start = DEG_BASE[g] + parity * pad_len
            ph = high_ref[start : start + pad_len, skip:]
            pw = low_ref[start : start + pad_len, skip:]
            main = dot(both, ph, NT)
            spectrum = main[:16] + (main[16:] + dot(both[:16], pw, NT))
            degree = wave + parity + 2 * lane
            degree_f = degree.astype(f32)
            ratio = rate * (degree_f * (degree_f + 1.0) / float(NM * (NM + 1)))
            damped = spectrum * (-ratio / (1.0 + ratio)) * factor
            damped = jnp.where(degree < NM, damped, 0.0)
            both = stacked_parts(damped)
            main = dot(both, ph, NN)
            grid = main[:16] + (main[16:] + dot(both[:16], pw, NN))
            if skip:
                grid = jnp.concatenate([jnp.zeros((16, skip), f32), grid], axis=1)
            results.append(grid)
        for a in range(N_LAT):
            place = a if a < 8 else 15 - a
            offset = ROWS * place
            base = offset // TILE * TILE
            shift = offset % TILE
            width = TILE if shift <= 48 else 256
            even = results[0][:, base : base + width]
            odd = results[1][:, base : base + width]
            piece = even + odd if a < 8 else even - odd
            if shift:
                piece = pltpu.roll(piece, width - shift, 1)
            for f in range(FL):
                out_ref[a * 8 + f, g, :, :] = piece[2 * f : 2 * f + 2, :TILE]


def legendre_call(wave, coeff, high, low, weight, rate):
    vmem = pl.BlockSpec(memory_space=pltpu.VMEM)
    smem = pl.BlockSpec(memory_space=pltpu.SMEM)
    return pl.pallas_call(
        legendre_kernel,
        in_specs=[smem] + [vmem] * 5,
        out_specs=vmem,
        out_shape=jax.ShapeDtypeStruct((N_LAT * N_LON, GROUPS, 2, TILE), f32),
        scratch_shapes=[pltpu.VMEM((GROUPS, 16, 896), f32)] * 2
        + [pltpu.VMEM((2, 16, HALF), f32)],
        compiler_params=pltpu.CompilerParams(vmem_limit_bytes=VMEM),
        name="legendre",
    )(wave, coeff, high, low, weight, rate)


def synthesis_kernel(back_ref, real_high, real_low, mixed_high, mixed_low, synth, waves):
    for m1 in range(8):
        for h in range(N_LAT):
            for g in range(GROUPS):
                start = m1 * 160 + h * WAVE_DEV + 2 * g
                waves[start : start + 2, :] = back_ref[h * 8 + m1, g, :, :]

    def transform(parts, wh, wl):
        stacked = jnp.concatenate([waves[m1 * 160 : m1 * 160 + 160, :] for m1 in parts], axis=0)
        both = stacked_parts(stacked.T[:ROWS, :])
        main = dot(both, wh, NN)
        return main[:ROWS] + (main[ROWS:] + dot(both[:ROWS], wl, NN))

    for i, m1 in enumerate((0, 4)):
        synth[:, i * BAND : (i + 1) * BAND] = transform((m1,), real_high[i], real_low[i])
    for q in (1, 2, 3):
        synth[:, 2 * q * BAND : (2 * q + 2) * BAND] = transform(
            (q, 8 - q), mixed_high[q - 1], mixed_low[q - 1]
        )


def synthesis_call(back, tables):
    vmem = pl.BlockSpec(memory_space=pltpu.VMEM)
    return pl.pallas_call(
        synthesis_kernel,
        in_specs=[vmem] * 5,
        out_specs=vmem,
        out_shape=jax.ShapeDtypeStruct((ROWS, NLON), f32),
        scratch_shapes=[pltpu.VMEM((8 * 160, TILE), f32)],
        compiler_params=pltpu.CompilerParams(vmem_limit_bytes=VMEM),
        cost_estimate=pl.CostEstimate(
            flops=6 * 80 * 860_160, bytes_accessed=8_000_000, transcendentals=0
        ),
        name="wave_synthesis",
    )(back, *tables)


def combine_kernel(lon_ref, synth, own_ref, other_ref, mix_ref, *rest):
    outs, (out_ref, sems) = rest[:N_LON], rest[N_LON:]
    root = math.sqrt(0.5)

    def combine(chunk, _):
        row = pl.multiple_of(chunk * 16, 16)
        diag = mix_ref[0, pl.ds(row, 16), :]
        cross = mix_ref[1, pl.ds(row, 16), :]
        for k in range(TPR):
            y = [
                synth[pl.ds(row, 16), i * BAND + k * TILE : i * BAND + (k + 1) * TILE]
                for i in range(8)
            ]
            e0, e1 = y[0] + y[1], y[0] - y[1]
            r1, i1, r2, i2, r3, i3 = y[2:]
            even = (e0 + r2, e1 - i2, e0 - r2, e1 + i2)
            odd = (
                r1 + r3,
                ((r1 - i1) - (r3 + i3)) * root,
                i3 - i1,
                ((r3 - i3) - (r1 + i1)) * root,
            )
            for b in range(N_LON):
                at = pl.multiple_of((b * TPR + k) * ROWS + chunk * 16, 16)
                own = own_ref[pl.ds(at, 16), :]
                diffused = own + diag * own + cross * other_ref[pl.ds(at, 16), :]
                wave = even[b % 4] + odd[b % 4] if b < 4 else even[b % 4] - odd[b % 4]
                out_ref[pl.ds(at, 16), :] = diffused + wave
        return 0

    lax.fori_loop(0, ROWS // 16, combine, 0)
    exchange = [
        pltpu.make_async_copy(
            out_ref.at[pl.ds(pl.multiple_of((lon_ref[0] ^ k) * TILES, 8), TILES), :],
            outs[k],
            sems.at[k],
        )
        for k in range(N_LON)
    ]
    for copy in exchange:
        copy.start()
    for copy in exchange:
        copy.wait()


def combine_call(lon, synth, own, other, mix):
    vmem = pl.BlockSpec(memory_space=pltpu.VMEM)
    smem = pl.BlockSpec(memory_space=pltpu.SMEM)
    return pl.pallas_call(
        combine_kernel,
        in_specs=[smem] + [vmem] * 4,
        out_specs=[pl.BlockSpec(memory_space=pl.ANY)] * N_LON,
        out_shape=[jax.ShapeDtypeStruct((TILES, TILE), f32)] * N_LON,
        scratch_shapes=[
            pltpu.VMEM((DENSE, TILE), f32),
            pltpu.SemaphoreType.DMA((N_LON,)),
        ],
        compiler_params=pltpu.CompilerParams(vmem_limit_bytes=VMEM),
        name="combine",
    )(lon, synth, own, other, mix)


def place_kernel(south_ref, lon_ref, *rest):
    chunks, (out_hbm, rows_ref, out_ref, sems, out_sems) = rest[:N_LON], rest[N_LON:]
    south = south_ref[0]
    loads = [
        pltpu.make_async_copy(
            chunks[k],
            rows_ref.at[pl.ds(pl.multiple_of((lon_ref[0] ^ k) * TILES, 8), TILES), :],
            sems.at[k],
        )
        for k in range(N_LON)
    ]
    for copy in loads:
        copy.start()
    for copy in loads:
        copy.wait()

    def place(i, _):
        target = jnp.where(south == 1, ROWS - 1 - i, i)
        for k in range(TPR):
            out_ref[target, :, k * TILE : (k + 1) * TILE] = rows_ref[
                pl.ds(k * ROWS + i, FL, stride=TILES), :
            ]
        return 0

    block = 16
    stores = []
    for piece in range(ROWS // block):
        lax.fori_loop(piece * block, (piece + 1) * block, place, 0, unroll=8)
        first = jnp.where(south == 1, ROWS - (piece + 1) * block, piece * block)
        sent = pltpu.make_async_copy(
            out_ref.at[pl.ds(first, block)], out_hbm.at[pl.ds(first, block)], out_sems.at[piece]
        )
        sent.start()
        stores.append(sent)
    for copy in stores:
        copy.wait()


def place_call(south, lon, chunks):
    smem = pl.BlockSpec(memory_space=pltpu.SMEM)
    return pl.pallas_call(
        place_kernel,
        in_specs=[smem, smem] + [pl.BlockSpec(memory_space=pl.ANY)] * N_LON,
        out_specs=pl.BlockSpec(memory_space=pl.ANY),
        out_shape=jax.ShapeDtypeStruct((ROWS, FL, BAND), f32),
        scratch_shapes=[
            pltpu.VMEM((FL * TILES, TILE), f32),
            pltpu.VMEM((ROWS, FL, BAND), f32),
            pltpu.SemaphoreType.DMA((N_LON,)),
            pltpu.SemaphoreType.DMA((ROWS // 16,)),
        ],
        compiler_params=pltpu.CompilerParams(vmem_limit_bytes=VMEM),
        name="place_rows",
    )(south, lon, *chunks)


def local(
    adjoint_grid, tile_owner, tile_slot, stencil, interp_weight, vertical_offset, diffusion_rate
):
    lat_here = lax.axis_index("lat")
    lon_here = lax.axis_index("lon")
    is_south = lat_here >= N_LAT // 2
    south = is_south.astype(jnp.int32).reshape(1)
    wave = (lon_here + 8 * lat_here).astype(jnp.int32)

    mix = vertical_offset.reshape(ROWS, 16)
    mix = jnp.where(is_south, jnp.flip(mix, 0), mix).T
    level = lon_here % 2
    field = lon_here // 2
    own_row = lax.dynamic_index_in_dim(mix, field * 4 + level * 3, 0, False)
    cross_row = lax.dynamic_index_in_dim(mix, field * 4 + (1 - level) * 2 + level, 0, False)
    blend = jnp.stack([own_row, cross_row])
    mix_grid = jnp.broadcast_to(blend[:, :, None], (2, ROWS, TILE))
    extra = blend.reshape(2, GROUPS, 16).transpose(1, 0, 2).reshape(WAVE_DEV, 16)
    extra = jnp.pad(jnp.tile(extra, (N_LAT, 1)), ((0, 0), (TILE - 16, 0)))

    latitude = 0.5 * math.pi - math.pi * (np.arange(HALF) + 0.5) / NLAT
    sine = jnp.asarray(np.sin(latitude)[None, :], f32)
    logcos = jnp.asarray(np.log(np.cos(latitude))[None, :], f32)
    weight = jnp.asarray((math.pi / NLAT * np.cos(latitude) / NLON)[None, :], f32)
    groups = np.zeros((TILE, 8))
    groups[:, :GROUPS] = log_norms().reshape(GROUPS, TILE).T
    norm = lax.dynamic_index_in_dim(jnp.asarray(groups, f32), wave, 0, False)
    norm = jnp.broadcast_to(norm[:, None], (8, TILE))
    group_start = jnp.minimum(jnp.arange(8, dtype=jnp.int32), GROUPS - 1) * TILE
    order = jnp.broadcast_to((wave + group_start).astype(f32)[:, None], (8, TILE))
    rate = jnp.broadcast_to(
        jnp.repeat(diffusion_rate, 2, total_repeat_length=16)[:, None], (16, TILE)
    )
    real, mixed = wave_tables()
    tables = tuple(jnp.asarray(part) for part in two_parts(real) + two_parts(mixed))

    lon = lon_here.astype(jnp.int32).reshape(1)

    def exchanged(chunks):
        return [chunks[0]] + [
            lax.ppermute(chunks[k], "lon", [(i, i ^ k) for i in range(N_LON)])
            for k in range(1, N_LON)
        ]

    chunks = exchanged(spread_call(
        jnp.stack([lon_here, lat_here]).astype(jnp.int32),
        adjoint_grid,
        stencil,
        interp_weight,
        tile_owner.reshape(1, TILES),
        tile_slot.reshape(1, TILES),
    ))
    high, low = table_call(order, norm, sine, logcos)
    tables, high, low, extra, rate, mix_grid = lax.optimization_barrier(
        (tables, high, low, extra, rate, mix_grid)
    )
    dense_below, dense_here, dense_above, coeff = fourier_call(south, chunks, tables, extra)
    coeff = lax.all_to_all(coeff, ("lat", "lon"), 0, 0, tiled=True)
    below = lax.ppermute(dense_below, "lat", [(i + 1, i) for i in range(N_LAT - 1)])
    above = lax.ppermute(dense_above, "lat", [(i, i + 1) for i in range(N_LAT - 1)])
    back = legendre_call(wave.reshape(1), coeff, high, low, weight, rate)
    back = lax.all_to_all(back, ("lat", "lon"), 0, 0, tiled=True)
    dense_here, back = lax.optimization_barrier((dense_here, back))
    departed = dense_here + below + above
    other = lax.ppermute(departed, "lon", [(i, i ^ 1) for i in range(N_LON)])
    synth = synthesis_call(back, tables)
    result = exchanged(combine_call(lon, synth, departed, other, mix_grid))
    return place_call(south, lon, result)


def solution(mesh):
    in_specs = (
        P("lat", None, "lon"),
        P("lat", "lon", None, None),
        P("lat", "lon", None, None),
        P("lat", "lon", None, None),
        P("lat", "lon", None, None),
        P("lat", None, None, None),
        P(),
    )
    out_specs = P("lat", None, "lon")
    return jax.shard_map(local, mesh=mesh, in_specs=in_specs, out_specs=out_specs, check_vma=False)
```

```python
import math

import jax
import jax.numpy as jnp
import ml_dtypes
import numpy as np
from jax import lax
from jax.experimental import pallas as pl
from jax.experimental.pallas import tpu as pltpu
from jax.sharding import PartitionSpec as P

NLAT = 1280
NLON = 3072
NM = 640
FL = 8
STEN = 4
TILE = 128
ROWS = 80
TPR = 3
TILES = 240
N_LAT = 16
N_LON = 8
HALF = NLAT // 2
BAND = NLON // N_LON
GROUPS = 5
WAVE_DEV = 2 * GROUPS
DENSE = N_LON * TPR * ROWS
CHUNK = TILES + 8
CHAINS = 4
DEG_PAD = (320, 256, 192, 128, 64)
DEG_USED = (320, 256, 192, 128, 64)
DEG_BASE = (0, 640, 1152, 1536, 1792)
DEG_TOTAL = 1920
VMEM = 40 * 1024 * 1024
VMEM_LARGE = 60 * 1024 * 1024

f32 = jnp.float32
bf16 = jnp.bfloat16
NT = (((1,), (1,)), ((), ()))
NN = (((1,), (0,)), ((), ()))


def two_parts(values):
    high = values.astype(ml_dtypes.bfloat16)
    low = (values - high.astype(np.float64)).astype(ml_dtypes.bfloat16)
    return high, low


def wave_tables():
    h = np.arange(N_LAT)[:, None]
    g = np.arange(GROUPS)[None, :]
    points = np.arange(BAND)

    def angle(m1):
        waves = (m1 + 8 * h + 128 * g).reshape(-1)
        return (waves[:, None] * points[None, :] % NLON) * (2.0 * math.pi / NLON)

    def rows(first, second):
        return np.stack([first, second], axis=1).reshape(-1, first.shape[-1])

    real = np.stack([rows(np.cos(angle(m1)), -np.sin(angle(m1))) for m1 in (0, 4)])
    mixed = []
    for q in (1, 2, 3):
        a, b = angle(q), angle(8 - q)
        upper = rows(
            np.concatenate([np.cos(a), np.sin(a)], 1), np.concatenate([-np.sin(a), np.cos(a)], 1)
        )
        lower = rows(
            np.concatenate([np.cos(b), -np.sin(b)], 1),
            np.concatenate([-np.sin(b), -np.cos(b)], 1),
        )
        mixed.append(np.concatenate([upper, lower], 0))
    return real, np.stack(mixed)


def log_norms():
    return np.array(
        [
            0.5 * (math.lgamma(m + 1.5) - math.lgamma(m + 1.0) - 0.5 * math.log(math.pi))
            for m in range(NM)
        ]
    )


def first_lanes():
    latitude = 0.5 * math.pi - math.pi * (np.arange(HALF) + 0.5) / NLAT
    exponent = log_norms()[:, None] + np.arange(NM)[:, None] * np.log(np.cos(latitude))[None, :]
    firsts = np.argmax(exponent >= -61.0, axis=1).reshape(GROUPS, NM // GROUPS).min(axis=1)
    return [int(first) // TILE * TILE for first in firsts]


LANES = first_lanes()


def split(values):
    high = values.astype(bf16)
    low = (values - high.astype(f32)).astype(bf16)
    return high, low


def stacked_parts(values):
    high = values.astype(bf16).astype(f32)
    return jnp.concatenate([high, values - high], axis=0).astype(bf16)


def dot(a, b, dims):
    return lax.dot_general(a, b, dims, preferred_element_type=f32)


def spread_kernel(lon_ref, grid_ref, stencil_ref, weight_ref, owner_ref, slot_ref, *rest):
    outs, (out_ref, sems) = rest[:N_LON], rest[N_LON:]
    block = grid_ref.shape[0]
    step = pl.program_id(0)
    target = lax.broadcasted_iota(jnp.int32, (TILE, TILE), 0).astype(jnp.int16)

    def tall(row, kind):
        block16 = jnp.broadcast_to(row, (16, TILE)).astype(kind)
        return jnp.concatenate([block16] * (TILE // 16), axis=0)

    for r in range(block):
        for k in range(TPR):
            field = grid_ref[r, :, k * TILE : (k + 1) * TILE]
            points = [stencil_ref[r, k, s : s + 1, :] for s in range(STEN)]
            weights = [weight_ref[r, k, s : s + 1, :] for s in range(STEN)]
            for s in range(STEN):
                for later in range(s + 1, STEN):
                    weights[s] = weights[s] + jnp.where(
                        points[later] == points[s], weight_ref[r, k, later : later + 1, :], 0.0
                    )
            high = jnp.zeros((TILE, TILE), bf16)
            low = high
            for s in reversed(range(STEN)):
                top = weights[s].astype(bf16).astype(f32)
                here = tall(points[s], jnp.int16) == target
                high = jnp.where(here, tall(top, bf16), high)
                low = jnp.where(here, tall(weights[s] - top, bf16), low)
            top = field.astype(bf16).astype(f32)
            sides = jnp.concatenate(
                [
                    jnp.concatenate([top, field - top], axis=0),
                    jnp.concatenate([top, jnp.zeros_like(top)], axis=0),
                ],
                axis=1,
            ).astype(bf16)
            both = dot(sides, jnp.concatenate([high, low], axis=1), NT)
            tile = step * (block * TPR) + r * TPR + k
            out_ref[pl.ds(tile, FL, stride=CHUNK), :] = both[:FL] + both[FL:]

    @pl.when(step == pl.num_programs(0) - 1)
    def _():
        owner, slot = owner_ref[...], slot_ref[...]
        dest_lat = owner // N_LON
        line = (slot * 171) // 512
        column = (owner - dest_lat * N_LON) * TPR + slot - line * TPR
        line = jnp.where(dest_lat >= N_LAT // 2, ROWS - 1 - line, line)
        keys = ((dest_lat - lon_ref[1] + 1) * (N_LON * TPR) + column) * ROWS + line
        keys = keys.astype(f32)
        for f in range(FL):
            at = f * CHUNK + TILES
            out_ref[at : at + 8, :] = jnp.zeros((8, TILE), f32)
            out_ref[at : at + 1, :] = keys[:, :TILE]
            out_ref[at + 1 : at + 2, : TILES - TILE] = keys[:, TILE:]
        exchange = [
            pltpu.make_async_copy(
                out_ref.at[pl.ds(pl.multiple_of((lon_ref[0] ^ k) * CHUNK, 8), CHUNK), :],
                outs[k],
                sems.at[k],
            )
            for k in range(N_LON)
        ]
        for copy in exchange:
            copy.start()
        for copy in exchange:
            copy.wait()


def spread_call(lon, grid, stencil, weight, owner, slot):
    block = 40
    return pl.pallas_call(
        spread_kernel,
        grid=(ROWS // block,),
        in_specs=[
            pl.BlockSpec(memory_space=pltpu.SMEM),
            pl.BlockSpec((block, FL, BAND), lambda i: (i, 0, 0)),
            pl.BlockSpec((block, TPR, STEN, TILE), lambda i: (i, 0, 0, 0)),
            pl.BlockSpec((block, TPR, STEN, TILE), lambda i: (i, 0, 0, 0)),
            pl.BlockSpec((1, TILES), lambda i: (0, 0)),
            pl.BlockSpec((1, TILES), lambda i: (0, 0)),
        ],
        out_specs=[pl.BlockSpec(memory_space=pl.ANY)] * N_LON,
        out_shape=[jax.ShapeDtypeStruct((CHUNK, TILE), f32)] * N_LON,
        scratch_shapes=[
            pltpu.VMEM((FL * CHUNK, TILE), f32),
            pltpu.SemaphoreType.DMA((N_LON,)),
        ],
        compiler_params=pltpu.CompilerParams(vmem_limit_bytes=VMEM_LARGE),
        name="spread",
    )(lon, grid, stencil, weight, owner, slot)


def table_kernel(order_ref, norm_ref, sine_ref, logcos_ref, high_ref, low_ref, ring):
    order = order_ref[...]
    order_wide = jnp.concatenate([order] * GROUPS, axis=1)
    norm_wide = jnp.concatenate([norm_ref[...]] * GROUPS, axis=1)
    sine = jnp.broadcast_to(sine_ref[...], (8, HALF))
    exponent = norm_wide + order_wide * logcos_ref[...]
    kept = exponent >= -60.0
    diagonal = jnp.where(kept, jnp.exp(jnp.where(kept, exponent, 0.0)), 0.0)
    order_sq = order * order

    def scale_of(degree):
        return jnp.sqrt(
            jnp.maximum(4.0 * degree * degree - 1.0, 1.0)
            / jnp.maximum(degree * degree - order_sq, 1.0)
        )

    def advance(block, carried):
        previous, earlier, scale_prev = carried
        for local in range(32):
            degree = order + (block * 32 + local).astype(f32)
            scale = scale_of(degree)
            ratio = scale / scale_prev
            wide = jnp.concatenate([scale] * GROUPS, axis=1)
            wide_ratio = jnp.concatenate([ratio] * GROUPS, axis=1)
            stepped = (wide * sine) * previous - wide_ratio * earlier
            if local == 0:
                stepped = jnp.where(block == 0, diagonal, stepped)
            slot = (local % 2) * 16 + local // 2
            for v in range(GROUPS):
                at = v * 256 + slot * 8
                ring[at : at + 8, :] = stepped[:, v * TILE : (v + 1) * TILE]
            earlier = previous
            previous = stepped
            scale_prev = scale
        for g in range(GROUPS):

            @pl.when(block * 16 < DEG_USED[g])
            def _():
                for parity in range(2):
                    rows = jnp.concatenate(
                        [
                            ring[pl.ds(v * 256 + parity * 128 + g, 16, stride=8), :]
                            for v in range(GROUPS)
                        ],
                        axis=1,
                    )
                    high, low = split(rows)
                    start = pl.multiple_of(
                        DEG_BASE[g] + parity * DEG_PAD[g] + block * 16, 16
                    )
                    high_ref[pl.ds(start, 16), :] = high
                    low_ref[pl.ds(start, 16), :] = low

        return previous, earlier, scale_prev

    for g in range(GROUPS):
        extra = DEG_PAD[g] - DEG_USED[g]
        if extra:
            for parity in range(2):
                start = DEG_BASE[g] + parity * DEG_PAD[g] + DEG_USED[g]
                high_ref[start : start + extra, :] = jnp.zeros((extra, HALF), bf16)
                low_ref[start : start + extra, :] = jnp.zeros((extra, HALF), bf16)
    blank = jnp.zeros((8, HALF), f32)
    lax.fori_loop(0, NM // 32, advance, (blank, blank, jnp.ones((8, TILE), f32)))


def table_call(order, norm, sine, logcos):
    shape = jax.ShapeDtypeStruct((DEG_TOTAL, HALF), bf16)
    return pl.pallas_call(
        table_kernel,
        out_shape=(shape, shape),
        scratch_shapes=[pltpu.VMEM((GROUPS * 256, TILE), f32)],
        compiler_params=pltpu.CompilerParams(vmem_limit_bytes=VMEM),
        cost_estimate=pl.CostEstimate(
            flops=640 * 5120 * 20, bytes_accessed=6_000_000, transcendentals=640 * 2048
        ),
        name="legendre_table",
    )(order, norm, sine, logcos)


def fourier_kernel(south_ref, extra_ref, *refs):
    chunks = refs[:N_LON]
    stored = refs[N_LON : N_LON + 4]
    bands = refs[N_LON + 4 : N_LON + 7]
    out_hbm = refs[N_LON + 7]
    scratch = refs[N_LON + 8 :]
    sums = scratch[:CHAINS]
    c_high, c_low, tiles, lines, whole, keys, dense_ref, out_ref = scratch[CHAINS : CHAINS + 8]
    tables = scratch[CHAINS + 8 : CHAINS + 12]
    key_sems, tile_sems, table_sems, band_sems, out_sems = scratch[CHAINS + 12 :]
    real_high, real_low, mixed_high, mixed_low = tables
    key_loads = [
        pltpu.make_async_copy(
            chunks[k].at[pl.ds(TILES, 8), :], lines.at[pl.ds(8 * k, 8), :], key_sems.at[k]
        )
        for k in range(N_LON)
    ]
    tile_loads = [
        pltpu.make_async_copy(chunks[k].at[pl.ds(0, TILES), :], tiles.at[k], tile_sems.at[k])
        for k in range(N_LON)
    ]
    table_loads = [
        pltpu.make_async_copy(stored[i], tables[i], table_sems.at[i]) for i in range(4)
    ]
    for copy in key_loads + tile_loads + table_loads:
        copy.start()
    for copy in key_loads:
        copy.wait()
    whole[...] = lines[...].astype(jnp.int32)
    to_scalars = pltpu.make_async_copy(whole, keys, key_sems.at[N_LON])
    to_scalars.start()
    for chain in sums:
        chain[...] = jnp.zeros(chain.shape, f32)
    to_scalars.wait()
    for copy in tile_loads:
        copy.wait()
    share = N_LON // CHAINS
    for part in range(share):
        for line, count in ((0, TILE), (1, TILES - TILE)):

            def scatter(t, _):
                for c, chain in enumerate(sums):
                    k = c * share + part
                    slot = keys[8 * k + line, t]
                    tile = tiles[k, pl.ds(line * TILE + t, 1), :]
                    chain[pl.ds(slot, 1), :] = chain[pl.ds(slot, 1), :] + tile
                return 0

            lax.fori_loop(0, count, scatter, 0, unroll=16)
    south = south_ref[0]
    root = math.sqrt(0.5)
    blank = jnp.zeros((16, NLON), bf16)
    c_high[240:256, :] = blank
    c_low[240:256, :] = blank

    def butterfly(band, chunk):
        place = jnp.where(south == 1, 2 - band, band)
        row = pl.multiple_of(place * ROWS + chunk * 16, 16)

        def put(column, values):
            high, low = split(values)
            c_high[pl.ds(row, 16), column : column + TILE] = high
            c_low[pl.ds(row, 16), column : column + TILE] = low

        for k in range(TPR):
            d = []
            for b in range(N_LON):
                start = pl.multiple_of(
                    band * DENSE + (b * TPR + k) * ROWS + chunk * 16, 16
                )
                total = sums[0][pl.ds(start, 16), :]
                for chain in sums[1:]:
                    total = total + chain[pl.ds(start, 16), :]
                dense_ref[pl.ds(start, 16), :] = total
                d.append(total)
            s = [d[i] + d[i + 4] for i in range(4)]
            t = [d[i] - d[i + 4] for i in range(4)]
            even, odd = s[0] + s[2], s[1] + s[3]
            minus = (t[1] - t[3]) * root
            plus = (t[1] + t[3]) * root
            at = k * TILE
            put(at, even + odd)
            put(BAND + at, even - odd)
            put(2 * BAND + at, t[0] + minus)
            put(3 * BAND + at, -t[2] - plus)
            put(4 * BAND + at, s[0] - s[2])
            put(5 * BAND + at, s[3] - s[1])
            put(6 * BAND + at, t[0] - minus)
            put(7 * BAND + at, t[2] - plus)

    stores = []
    for band in range(3):

        def step(chunk, _, band=band):
            butterfly(band, chunk)
            return 0

        lax.fori_loop(0, ROWS // 16, step, 0)
        sent = pltpu.make_async_copy(
            dense_ref.at[pl.ds(band * DENSE, DENSE), :], bands[band], band_sems.at[band]
        )
        sent.start()
        stores.append(sent)
    extra = extra_ref[...]
    for copy in table_loads:
        copy.wait()

    def emit(m1, block):
        block = jnp.concatenate([block[:, :TILE], block[:, TILE:] + extra], axis=1)
        for h in range(N_LAT):
            for g in range(GROUPS):
                start = h * WAVE_DEV + 2 * g
                out_ref[m1, h, g, :, :] = block[start : start + 2, :]
        sent = pltpu.make_async_copy(out_ref.at[m1], out_hbm.at[:, m1], out_sems.at[m1])
        sent.start()
        stores.append(sent)

    def transform(ch, cl, wh, wl):
        rows = wh.shape[0]
        both = dot(jnp.concatenate([wh, wl], axis=0), ch, NT)
        return both[:rows] + (both[rows:] + dot(wh, cl, NT))

    for i, m1 in enumerate((0, 4)):
        at = slice(i * BAND, (i + 1) * BAND)
        emit(m1, transform(c_high[:, at], c_low[:, at], real_high[i], real_low[i]))
    for q in (1, 2, 3):
        at = slice(2 * q * BAND, (2 * q + 2) * BAND)
        pair = transform(c_high[:, at], c_low[:, at], mixed_high[q - 1], mixed_low[q - 1])
        emit(q, pair[:160])
        emit(8 - q, pair[160:])
    for copy in stores:
        copy.wait()


def fourier_call(south, chunks, tables, extra):
    vmem = pl.BlockSpec(memory_space=pltpu.VMEM)
    smem = pl.BlockSpec(memory_space=pltpu.SMEM)
    anywhere = pl.BlockSpec(memory_space=pltpu.HBM)
    result = pl.pallas_call(
        fourier_kernel,
        in_specs=[smem, vmem] + [anywhere] * (N_LON + 4),
        out_specs=[anywhere] * 4,
        out_shape=[jax.ShapeDtypeStruct((DENSE, TILE), f32)] * 3
        + [jax.ShapeDtypeStruct((N_LAT, N_LON, GROUPS, 2, 256), f32)],
        scratch_shapes=[pltpu.VMEM((3 * DENSE, TILE), f32)] * CHAINS
        + [pltpu.VMEM((256, NLON), bf16)] * 2
        + [
            pltpu.VMEM((N_LON, TILES, TILE), f32),
            pltpu.VMEM((8 * N_LON, TILE), f32),
            pltpu.VMEM((8 * N_LON, TILE), jnp.int32),
            pltpu.SMEM((8 * N_LON, TILE), jnp.int32),
            pltpu.VMEM((3 * DENSE, TILE), f32),
            pltpu.VMEM((N_LON, N_LAT, GROUPS, 2, 256), f32),
        ]
        + [pltpu.VMEM(table.shape, table.dtype) for table in tables]
        + [
            pltpu.SemaphoreType.DMA((N_LON + 1,)),
            pltpu.SemaphoreType.DMA((N_LON,)),
            pltpu.SemaphoreType.DMA((4,)),
            pltpu.SemaphoreType.DMA((3,)),
            pltpu.SemaphoreType.DMA((N_LON,)),
        ],
        compiler_params=pltpu.CompilerParams(vmem_limit_bytes=50 * 1024 * 1024),
        name="scatter_fourier",
    )(south, extra, *chunks, *tables)
    return list(result[:3]) + [result[3].reshape(N_LAT * N_LON, GROUPS, 2, 256)]


def legendre_kernel(
    wave_ref, coeff_ref, high_ref, low_ref, weight_ref, rate_ref, out_ref, north, south, blend
):
    weight = weight_ref[...]
    row16 = lax.broadcasted_iota(jnp.int32, (16, HALF), 0)
    first_level = (row16 // 2) % 2 == 0
    is_first = row16 % 2 == 0
    lane128 = lax.broadcasted_iota(jnp.int32, (16, TILE), 1)
    is_blend = lane128 >= TILE - 16

    def mixed(values, own, cross):
        ahead = pltpu.roll(values, 14, 0)
        behind = pltpu.roll(values, 2, 0)
        other = jnp.where(first_level, ahead, behind)
        return values + own * values + cross * other

    pad = jnp.zeros((16, TILE), f32)
    north[...] = jnp.zeros(north.shape, f32)
    south[...] = jnp.zeros(south.shape, f32)
    blend[...] = jnp.zeros(blend.shape, f32)
    for g in range(GROUPS):
        for a in range(N_LAT):
            total, place = (north, a) if a < 8 else (south, 15 - a)
            piece = jnp.concatenate([coeff_ref[a * 8 + f, g, :, :] for f in range(FL)], axis=0)
            last = piece[:, TILE:]
            piece = jnp.concatenate([piece[:, :TILE], jnp.where(is_blend, 0.0, last), pad], axis=1)
            offset = ROWS * place + 48
            base = offset // TILE * TILE
            total[g, :, base : base + 384] += pltpu.roll(piece, offset % TILE, 1)
            offset = ROWS * place + 16 * g
            base = offset // TILE * TILE
            last = pltpu.roll(jnp.where(is_blend, last, 0.0), (offset % TILE + 16) % TILE, 1)
            blend[a // 8, :, base : base + TILE] += last
    blends = []
    for side in range(2):
        both = blend[side]
        blends.append(jnp.where(is_first, both, pltpu.roll(both, 1, 0)))
        blends.append(jnp.where(is_first, pltpu.roll(both, 15, 0), both))
    dn, xn, ds, xs = blends
    for g in range(GROUPS):
        extra_n = north[g, :, 768:896]
        extra_s = south[g, :, 768:896]
        north[g, :, 640:768] += pltpu.roll(extra_s, 48, 1)
        south[g, :, 640:768] += pltpu.roll(extra_n, 48, 1)
        full_n = mixed(north[g, :, 128:768], dn, xn)
        full_s = mixed(south[g, :, 128:768], ds, xs)
        pad_len = DEG_PAD[g]
        wave = wave_ref[0] + 128 * g
        factor = jnp.where(wave == 0, 1.0, 2.0).astype(f32)
        lane = lax.broadcasted_iota(jnp.int32, (16, pad_len), 1)
        rate = jnp.concatenate([rate_ref[...]] * (-(-pad_len // TILE)), axis=1)[:, :pad_len]
        results = []
        for parity, folded in enumerate((full_n + full_s, full_n - full_s)):
            skip = LANES[g]
            both = stacked_parts((folded * weight)[:, skip:])
            start = DEG_BASE[g] + parity * pad_len
            ph = high_ref[start : start + pad_len, skip:]
            pw = low_ref[start : start + pad_len, skip:]
            main = dot(both, ph, NT)
            spectrum = main[:16] + (main[16:] + dot(both[:16], pw, NT))
            degree = wave + parity + 2 * lane
            degree_f = degree.astype(f32)
            ratio = rate * (degree_f * (degree_f + 1.0) / float(NM * (NM + 1)))
            damped = spectrum * (-ratio / (1.0 + ratio)) * factor
            damped = jnp.where(degree < NM, damped, 0.0)
            both = stacked_parts(damped)
            main = dot(both, ph, NN)
            grid = main[:16] + (main[16:] + dot(both[:16], pw, NN))
            if skip:
                grid = jnp.concatenate([jnp.zeros((16, skip), f32), grid], axis=1)
            results.append(grid)
        for a in range(N_LAT):
            place = a if a < 8 else 15 - a
            offset = ROWS * place
            base = offset // TILE * TILE
            shift = offset % TILE
            width = TILE if shift <= 48 else 256
            even = results[0][:, base : base + width]
            odd = results[1][:, base : base + width]
            piece = even + odd if a < 8 else even - odd
            if shift:
                piece = pltpu.roll(piece, width - shift, 1)
            for f in range(FL):
                out_ref[a * 8 + f, g, :, :] = piece[2 * f : 2 * f + 2, :TILE]


def legendre_call(wave, coeff, high, low, weight, rate):
    vmem = pl.BlockSpec(memory_space=pltpu.VMEM)
    smem = pl.BlockSpec(memory_space=pltpu.SMEM)
    return pl.pallas_call(
        legendre_kernel,
        in_specs=[smem] + [vmem] * 5,
        out_specs=vmem,
        out_shape=jax.ShapeDtypeStruct((N_LAT * N_LON, GROUPS, 2, TILE), f32),
        scratch_shapes=[pltpu.VMEM((GROUPS, 16, 896), f32)] * 2
        + [pltpu.VMEM((2, 16, HALF), f32)],
        compiler_params=pltpu.CompilerParams(vmem_limit_bytes=VMEM),
        name="legendre",
    )(wave, coeff, high, low, weight, rate)


def synthesis_kernel(back_ref, real_high, real_low, mixed_high, mixed_low, synth, waves):
    for m1 in range(8):
        for h in range(N_LAT):
            for g in range(GROUPS):
                start = m1 * 160 + h * WAVE_DEV + 2 * g
                waves[start : start + 2, :] = back_ref[h * 8 + m1, g, :, :]

    def transform(parts, wh, wl):
        stacked = jnp.concatenate([waves[m1 * 160 : m1 * 160 + 160, :] for m1 in parts], axis=0)
        both = stacked_parts(stacked.T[:ROWS, :])
        main = dot(both, wh, NN)
        return main[:ROWS] + (main[ROWS:] + dot(both[:ROWS], wl, NN))

    for i, m1 in enumerate((0, 4)):
        synth[:, i * BAND : (i + 1) * BAND] = transform((m1,), real_high[i], real_low[i])
    for q in (1, 2, 3):
        synth[:, 2 * q * BAND : (2 * q + 2) * BAND] = transform(
            (q, 8 - q), mixed_high[q - 1], mixed_low[q - 1]
        )


def synthesis_call(back, tables):
    vmem = pl.BlockSpec(memory_space=pltpu.VMEM)
    return pl.pallas_call(
        synthesis_kernel,
        in_specs=[vmem] * 5,
        out_specs=vmem,
        out_shape=jax.ShapeDtypeStruct((ROWS, NLON), f32),
        scratch_shapes=[pltpu.VMEM((8 * 160, TILE), f32)],
        compiler_params=pltpu.CompilerParams(vmem_limit_bytes=VMEM),
        cost_estimate=pl.CostEstimate(
            flops=6 * 80 * 860_160, bytes_accessed=8_000_000, transcendentals=0
        ),
        name="wave_synthesis",
    )(back, *tables)


def combine_kernel(lon_ref, synth, own_ref, other_ref, mix_ref, *rest):
    outs, (out_ref, sems) = rest[:N_LON], rest[N_LON:]
    root = math.sqrt(0.5)

    def combine(chunk, _):
        row = pl.multiple_of(chunk * 16, 16)
        diag = mix_ref[0, pl.ds(row, 16), :]
        cross = mix_ref[1, pl.ds(row, 16), :]
        for k in range(TPR):
            y = [
                synth[pl.ds(row, 16), i * BAND + k * TILE : i * BAND + (k + 1) * TILE]
                for i in range(8)
            ]
            e0, e1 = y[0] + y[1], y[0] - y[1]
            r1, i1, r2, i2, r3, i3 = y[2:]
            even = (e0 + r2, e1 - i2, e0 - r2, e1 + i2)
            odd = (
                r1 + r3,
                ((r1 - i1) - (r3 + i3)) * root,
                i3 - i1,
                ((r3 - i3) - (r1 + i1)) * root,
            )
            for b in range(N_LON):
                at = pl.multiple_of((b * TPR + k) * ROWS + chunk * 16, 16)
                own = own_ref[pl.ds(at, 16), :]
                diffused = own + diag * own + cross * other_ref[pl.ds(at, 16), :]
                wave = even[b % 4] + odd[b % 4] if b < 4 else even[b % 4] - odd[b % 4]
                out_ref[pl.ds(at, 16), :] = diffused + wave
        return 0

    lax.fori_loop(0, ROWS // 16, combine, 0)
    exchange = [
        pltpu.make_async_copy(
            out_ref.at[pl.ds(pl.multiple_of((lon_ref[0] ^ k) * TILES, 8), TILES), :],
            outs[k],
            sems.at[k],
        )
        for k in range(N_LON)
    ]
    for copy in exchange:
        copy.start()
    for copy in exchange:
        copy.wait()


def combine_call(lon, synth, own, other, mix):
    vmem = pl.BlockSpec(memory_space=pltpu.VMEM)
    smem = pl.BlockSpec(memory_space=pltpu.SMEM)
    return pl.pallas_call(
        combine_kernel,
        in_specs=[smem] + [vmem] * 4,
        out_specs=[pl.BlockSpec(memory_space=pl.ANY)] * N_LON,
        out_shape=[jax.ShapeDtypeStruct((TILES, TILE), f32)] * N_LON,
        scratch_shapes=[
            pltpu.VMEM((DENSE, TILE), f32),
            pltpu.SemaphoreType.DMA((N_LON,)),
        ],
        compiler_params=pltpu.CompilerParams(vmem_limit_bytes=VMEM),
        name="combine",
    )(lon, synth, own, other, mix)


def place_kernel(south_ref, lon_ref, *rest):
    chunks, (out_hbm, rows_ref, out_ref, sems, out_sems) = rest[:N_LON], rest[N_LON:]
    south = south_ref[0]
    loads = [
        pltpu.make_async_copy(
            chunks[k],
            rows_ref.at[pl.ds(pl.multiple_of((lon_ref[0] ^ k) * TILES, 8), TILES), :],
            sems.at[k],
        )
        for k in range(N_LON)
    ]
    for copy in loads:
        copy.start()
    for copy in loads:
        copy.wait()

    def place(i, _):
        target = jnp.where(south == 1, ROWS - 1 - i, i)
        for k in range(TPR):
            out_ref[target, :, k * TILE : (k + 1) * TILE] = rows_ref[
                pl.ds(k * ROWS + i, FL, stride=TILES), :
            ]
        return 0

    block = 16
    stores = []
    for piece in range(ROWS // block):
        lax.fori_loop(piece * block, (piece + 1) * block, place, 0, unroll=8)
        first = jnp.where(south == 1, ROWS - (piece + 1) * block, piece * block)
        sent = pltpu.make_async_copy(
            out_ref.at[pl.ds(first, block)], out_hbm.at[pl.ds(first, block)], out_sems.at[piece]
        )
        sent.start()
        stores.append(sent)
    for copy in stores:
        copy.wait()


def place_call(south, lon, chunks):
    smem = pl.BlockSpec(memory_space=pltpu.SMEM)
    return pl.pallas_call(
        place_kernel,
        in_specs=[smem, smem] + [pl.BlockSpec(memory_space=pl.ANY)] * N_LON,
        out_specs=pl.BlockSpec(memory_space=pl.ANY),
        out_shape=jax.ShapeDtypeStruct((ROWS, FL, BAND), f32),
        scratch_shapes=[
            pltpu.VMEM((FL * TILES, TILE), f32),
            pltpu.VMEM((ROWS, FL, BAND), f32),
            pltpu.SemaphoreType.DMA((N_LON,)),
            pltpu.SemaphoreType.DMA((ROWS // 16,)),
        ],
        compiler_params=pltpu.CompilerParams(vmem_limit_bytes=VMEM),
        name="place_rows",
    )(south, lon, *chunks)


def local(
    adjoint_grid, tile_owner, tile_slot, stencil, interp_weight, vertical_offset, diffusion_rate
):
    lat_here = lax.axis_index("lat")
    lon_here = lax.axis_index("lon")
    is_south = lat_here >= N_LAT // 2
    south = is_south.astype(jnp.int32).reshape(1)
    wave = (lon_here + 8 * lat_here).astype(jnp.int32)

    mix = vertical_offset.reshape(ROWS, 16)
    mix = jnp.where(is_south, jnp.flip(mix, 0), mix).T
    level = lon_here % 2
    field = lon_here // 2
    own_row = lax.dynamic_index_in_dim(mix, field * 4 + level * 3, 0, False)
    cross_row = lax.dynamic_index_in_dim(mix, field * 4 + (1 - level) * 2 + level, 0, False)
    blend = jnp.stack([own_row, cross_row])
    mix_grid = jnp.broadcast_to(blend[:, :, None], (2, ROWS, TILE))
    extra = blend.reshape(2, GROUPS, 16).transpose(1, 0, 2).reshape(WAVE_DEV, 16)
    extra = jnp.pad(jnp.tile(extra, (N_LAT, 1)), ((0, 0), (TILE - 16, 0)))

    latitude = 0.5 * math.pi - math.pi * (np.arange(HALF) + 0.5) / NLAT
    sine = jnp.asarray(np.sin(latitude)[None, :], f32)
    logcos = jnp.asarray(np.log(np.cos(latitude))[None, :], f32)
    weight = jnp.asarray((math.pi / NLAT * np.cos(latitude) / NLON)[None, :], f32)
    groups = np.zeros((TILE, 8))
    groups[:, :GROUPS] = log_norms().reshape(GROUPS, TILE).T
    norm = lax.dynamic_index_in_dim(jnp.asarray(groups, f32), wave, 0, False)
    norm = jnp.broadcast_to(norm[:, None], (8, TILE))
    group_start = jnp.minimum(jnp.arange(8, dtype=jnp.int32), GROUPS - 1) * TILE
    order = jnp.broadcast_to((wave + group_start).astype(f32)[:, None], (8, TILE))
    rate = jnp.broadcast_to(
        jnp.repeat(diffusion_rate, 2, total_repeat_length=16)[:, None], (16, TILE)
    )
    real, mixed = wave_tables()
    tables = tuple(jnp.asarray(part) for part in two_parts(real) + two_parts(mixed))

    lon = lon_here.astype(jnp.int32).reshape(1)

    def exchanged(chunks):
        return [chunks[0]] + [
            lax.ppermute(chunks[k], "lon", [(i, i ^ k) for i in range(N_LON)])
            for k in range(1, N_LON)
        ]

    chunks = exchanged(spread_call(
        jnp.stack([lon_here, lat_here]).astype(jnp.int32),
        adjoint_grid,
        stencil,
        interp_weight,
        tile_owner.reshape(1, TILES),
        tile_slot.reshape(1, TILES),
    ))
    high, low = table_call(order, norm, sine, logcos)
    tables, high, low, extra, rate, mix_grid = lax.optimization_barrier(
        (tables, high, low, extra, rate, mix_grid)
    )
    dense_below, dense_here, dense_above, coeff = fourier_call(south, chunks, tables, extra)
    coeff = lax.all_to_all(coeff, ("lat", "lon"), 0, 0, tiled=True)
    below = lax.ppermute(dense_below, "lat", [(i + 1, i) for i in range(N_LAT - 1)])
    above = lax.ppermute(dense_above, "lat", [(i, i + 1) for i in range(N_LAT - 1)])
    back = legendre_call(wave.reshape(1), coeff, high, low, weight, rate)
    back = lax.all_to_all(back, ("lat", "lon"), 0, 0, tiled=True)
    dense_here, back = lax.optimization_barrier((dense_here, back))
    departed = dense_here + below + above
    other = lax.ppermute(departed, "lon", [(i, i ^ 1) for i in range(N_LON)])
    synth = synthesis_call(back, tables)
    result = exchanged(combine_call(lon, synth, departed, other, mix_grid))
    return place_call(south, lon, result)


def solution(mesh):
    in_specs = (
        P("lat", None, "lon"),
        P("lat", "lon", None, None),
        P("lat", "lon", None, None),
        P("lat", "lon", None, None),
        P("lat", "lon", None, None),
        P("lat", None, None, None),
        P(),
    )
    out_specs = P("lat", None, "lon")
    return jax.shard_map(local, mesh=mesh, in_specs=in_specs, out_specs=out_specs, check_vma=False)
```
